512 devices in a mesh: view: 8 (over y, x_lo), slab: 32 (over z, core), row: 2 (over x_hi).
Axes of the slice: x: 4 (x_hi: 2, x_lo: 2; x = x_hi * 2 + x_lo), y: 4, z: 16, core: 2. Of those that a mesh axis runs over, the one named last changes fastest.
Arguments:
- data: float32 [8, 256, 128, 256], P('view', 'slab', 'row'), may hold values from 0.2 to 5
- estimate: float32 [256, 128, 256], P('slab', 'row'), may hold values from 0.5 to 2
- profile: float32 [8, 3, 5], P('view'), may hold values from 0.1 to 1
- band: int32 [8, 3], P('view'), may hold values from 1 to 4, as said below
- axes_perm: int32 [8, 3], P('view'), may hold values from 0 to 2, each once within a row
Outputs:
- updated: float32 [256, 128, 256], P('slab', 'row')
The draws below stay inside these ranges and needn't reach their ends.
Inputs may be any that keep to these rules, and one draw needn't show every extreme that they name: Some view's detection band (profile 0) is exactly 4.
All inputs are finite; a program needn't handle non-finite values.
Results may differ from the reference program's by a relative error of at most 0.0001.
Values sent between devices are 32-bit elements; how exact they have to be, the bound alone decides.
No kernel may reach another device: no remote copies, remote signals or barrier semaphores. Data moves between devices by JAX's collectives and lax.ppermute only.
A program may use at most 64 MiB of HBM per device.

```python
import math
import jax
import jax.numpy as jnp
import numpy as np
from jax import lax

NX = 256
H = 4
PASSES = 3
NV = 8
NZ = 256
NY = 128


def draw_band(key, part):
    key = jax.random.fold_in(key, 7)
    first, second = jax.random.split(key)
    widths = jax.random.randint(first, (NV, 3), 1, H + 1, dtype=jnp.int32)
    chosen = jax.random.randint(second, (), 0, NV, dtype=jnp.int32)
    return widths.at[chosen, 0].set(H)


def steps_of(stream_key, dims, cuts, low, high):
    gain, own = 1.0, jax.random.fold_in(stream_key, 6)
    for dim, shards_of in cuts:
        draws = jnp.exp(jax.random.uniform(jax.random.fold_in(own, dim), (shards_of,), jnp.float32, low / len(cuts), high / len(cuts)))
        gain = gain * jnp.repeat(draws, dims[dim] // shards_of).reshape([-1 if axis == dim else 1 for axis in range(len(dims))])
    return gain


def setup_inputs(seed: int = 0) -> dict:
    splits = jax.random.split(jax.random.key(seed), 6)
    data = jnp.clip(jnp.exp(math.log(5.0) - 3.218876 * jax.random.uniform(splits[0], (NV, NZ, NY, NX), jnp.float32) ** steps_of(splits[0], (NV, NZ, NY, NX), ((0, 8), (1, 32), (2, 2)), -0.2, 0.2)), 0.2, 5.0)
    estimate = jnp.clip(jnp.exp(math.log(2.0) - 1.3862944 * jax.random.uniform(splits[1], (NZ, NY, NX), jnp.float32) ** steps_of(splits[1], (NZ, NY, NX), ((0, 32), (1, 2)), -0.2, 0.2)), 0.5, 2.0)
    profile = jnp.clip(jnp.exp(math.log(1.0) - 2.3025851 * jax.random.uniform(splits[2], (NV, 3, H + 1), jnp.float32) ** steps_of(splits[2], (NV, 3, H + 1), ((0, 8),), -0.2, 0.2)), 0.1, 1.0)
    band = draw_band(jax.random.fold_in(splits[5], 71), 0)
    axes_perm = jax.vmap(lambda own: jax.random.permutation(own, 3))(jax.random.split(splits[4], NV)).reshape((NV, 3)).astype(jnp.int32)
    return dict(data=data, estimate=estimate, profile=profile, band=band, axes_perm=axes_perm)


TAU = 0.05
EPS2 = 0.25

def kernels(prof, band_row, perm_row):
    width = prof.shape[1] - 1
    taps = np.abs(np.arange(-width, width + 1))
    select = perm_row[:, None] == jnp.arange(3, dtype=jnp.int32)[None, :]
    chosen = jnp.dot(select.astype(jnp.float32), prof, precision=lax.Precision.HIGHEST)
    reach = lax.optimization_barrier(jnp.sum(jnp.where(select, band_row[None, :], 0), axis=1))
    weights = chosen[:, taps] * (jnp.asarray(taps, dtype=jnp.int32)[None, :] <= reach[:, None]).astype(jnp.float32)
    return weights / lax.optimization_barrier(jnp.sum(weights, axis=1, keepdims=True))

def blur_valid(block, weights, axis_num, width):
    length = block.shape[axis_num] - 2 * width
    total = jnp.zeros(block.shape[:axis_num] + (length,) + block.shape[axis_num + 1:], jnp.float32)
    for offset in range(-width, width + 1):
        total = total + weights[axis_num, offset + width] * lax.slice_in_dim(block, width + offset, width + offset + length, axis=axis_num)
    return total

def blur_whole(volume, weights, width):
    for axis_num in range(3):
        pads = [(0, 0)] * 3
        pads[axis_num] = (width, width)
        volume = blur_valid(jnp.pad(volume, pads), weights, axis_num, width)
    return volume

def tv_step(padded, mask):
    base = padded[:-1, :-1, :-1]
    grad_z = padded[1:, :-1, :-1] - base
    grad_y = padded[:-1, 1:, :-1] - base
    grad_x = padded[:-1, :-1, 1:] - base
    scale = mask[:-1, :-1, :-1] / jnp.sqrt(grad_z * grad_z + grad_y * grad_y + grad_x * grad_x + EPS2)
    flux_z = grad_z * scale
    flux_y = grad_y * scale
    flux_x = grad_x * scale
    spread = flux_z[1:, 1:, 1:] - flux_z[:-1, 1:, 1:]
    spread = spread + flux_y[1:, 1:, 1:] - flux_y[1:, :-1, 1:]
    spread = spread + flux_x[1:, 1:, 1:] - flux_x[1:, 1:, :-1]
    return (padded[1:-1, 1:-1, 1:-1] + TAU * spread) * mask[1:-1, 1:-1, 1:-1]

def reference(data, estimate, profile, band, axes_perm):
    width = profile.shape[2] - 1
    views = data.shape[0]

    def add_view(index, total):
        weights = kernels(profile[index], band[index], axes_perm[index])
        blurred = blur_whole(estimate, weights, width)
        ratio = data[index] / blurred
        return total + blur_whole(ratio, weights, width)
    total = lax.fori_loop(0, views, add_view, jnp.zeros(estimate.shape, jnp.float32))
    field = estimate * (total * (1.0 / views))
    for step in range(PASSES):
        padded = jnp.pad(field, 1)
        mask = jnp.pad(jnp.ones(field.shape, jnp.float32), 1)
        field = tv_step(padded, mask)
    return field
```

```python
import functools

import jax
import jax.numpy as jnp
from jax import lax
from jax.experimental import pallas as pl
from jax.experimental.pallas import tpu as pltpu
from jax.sharding import PartitionSpec as P

PASSES = 3
TAU = 0.05
EPS2 = 0.25
WIDTH = 4
EST_STRIP = 16
DATA_STRIP = 8
TV_HALO = 3
VMEM = pl.BlockSpec(memory_space=pltpu.VMEM)
SMEM = pl.BlockSpec(memory_space=pltpu.SMEM)
F32 = jnp.float32
BF16 = jnp.bfloat16


def split(x):
    high = x.astype(BF16)
    return high, (x - high.astype(F32)).astype(BF16)


def dot3(a_high, a_low, b_high, b_low):
    dot = functools.partial(jnp.dot, preferred_element_type=F32)
    return dot(a_high, b_high) + (dot(a_low, b_high) + dot(a_high, b_low))


def weights_kernel(rows, place, band, perm, prof, taps_z, wx_h, wx_l, wy1_h, wy1_l, wy2_h, wy2_l):
    row = place[2]
    pitch = wy1_h.shape[0] // 3
    halo1, halo2 = pitch - rows, pitch - rows - DATA_STRIP

    def taps(axis, shape):
        k = perm[axis]
        reach = band[k]
        parts = [jnp.where(t <= reach, prof[k * (WIDTH + 1) + t], 0.0) for t in range(WIDTH + 1)]
        total = parts[0]
        for part in parts[1:]:
            total = total + 2.0 * part
        return [jnp.full(shape, part, F32) / jnp.full(shape, total, F32) for part in parts]

    def banded(axis, shape, distance, keep, high, low):
        small = (8, shape[1])
        for start in range(0, shape[0], 16):
            pieces = []
            for t, tap in enumerate(taps(axis, small)):
                pieces.append(jnp.concatenate([tap, tap], axis=0))
            i = start + lax.broadcasted_iota(jnp.int32, (16, shape[1]), 0)
            j = lax.broadcasted_iota(jnp.int32, (16, shape[1]), 1)
            d = jnp.abs(distance(i, j))
            value = jnp.zeros((16, shape[1]), F32)
            for t in range(WIDTH + 1):
                value = jnp.where((d == t) & keep(i, j), pieces[t], value)
            high[start : start + 16, :], low[start : start + 16, :] = split(value)

    for t, tap in enumerate(taps(0, taps_z.shape[1:])):
        taps_z[t] = tap
    banded(2, wx_h.shape, lambda i, j: i - j, lambda i, j: (i >= 0), wx_h, wx_l)

    def plane_of(i):
        return (i >= pitch).astype(jnp.int32) + (i >= 2 * pitch).astype(jnp.int32)

    def halo_place(i, strip):
        i = i - pitch * plane_of(i)
        return jnp.where((i >= rows) & (row == 1), i - rows - strip, i)

    def ascending(i):
        return i - pitch * plane_of(i) - DATA_STRIP * row

    def same(i, j):
        return plane_of(i) == plane_of(j)

    def used(i):
        return i - pitch * plane_of(i) < rows + DATA_STRIP

    banded(
        1,
        wy1_h.shape,
        lambda i, j: halo_place(i, DATA_STRIP) - halo_place(j, EST_STRIP),
        lambda i, j: same(i, j) & used(i),
        wy1_h,
        wy1_l,
    )
    banded(
        1,
        wy2_h.shape,
        lambda i, j: ascending(i) - halo_place(j, DATA_STRIP),
        lambda i, j: same(i, j) & used(i) & used(j),
        wy2_h,
        wy2_l,
    )


def blur_z(read, taps_z, lanes):
    total = taps_z[0] * read(WIDTH)
    for t in range(1, WIDTH + 1):
        total = total + taps_z[t] * (read(WIDTH - t) + read(WIDTH + t))
    return total


def views_kernel(
    slabs, place, est, data, strip, below, above, strip_below, strip_above,
    taps_z, wx_h, wx_l, wy1_h, wy1_l, wy2_h, wy2_l, out, flat1, ratio, flat2,
):
    planes, rows, lanes = est.shape
    slab = place[1]
    pitch = rows + EST_STRIP
    used = rows + DATA_STRIP
    wide = planes + 2 * WIDTH

    def est_plane(q, first, count):
        if q < planes:
            return below[q, first : first + count, :]
        if q < 2 * planes:
            return est[q - planes, first : first + count, :]
        return above[q - 2 * planes, first : first + count, :]

    def est_strip(q):
        ref = (strip_below, strip, strip_above)[q // planes]
        return ref[q % planes, 0:EST_STRIP, :]

    for p in range(wide):
        for first in range(0, rows, 16):
            flat1[p * pitch + first : p * pitch + first + 16, :] = blur_z(
                lambda t: est_plane(p + t, first, 16), taps_z, lanes
            )
        flat1[p * pitch + rows : (p + 1) * pitch, :] = blur_z(
            lambda t: est_strip(p + t), taps_z, lanes
        )

    def blur_yx(flat, start, count, w_h, w_l):
        n = count * pitch
        x_h, x_l = split(flat[start * pitch : start * pitch + n, :])
        mid = dot3(w_h[0:n, 0:n], w_l[0:n, 0:n], x_h, x_l)
        m_h, m_l = split(mid)
        return dot3(m_h, m_l, wx_h[...], wx_l[...])

    for start in range(0, wide, 3):
        count = min(3, wide - start)
        blurred = blur_yx(flat1, start, count, wy1_h, wy1_l)
        for p in range(start, start + count):
            own = blurred[(p - start) * pitch : (p - start) * pitch + rows, :]
            rim = blurred[(p - start) * pitch + rows : (p - start) * pitch + used, :]
            strip_rows = slice(EST_STRIP, EST_STRIP + DATA_STRIP)
            if p < WIDTH:
                top, low = below[planes + p], strip_below[planes - WIDTH + p, strip_rows, :]
                inside = slab > 0
            elif p < WIDTH + planes:
                top, low = data[p - WIDTH], strip[p - WIDTH, strip_rows, :]
                inside = None
            else:
                q = p - WIDTH - planes
                top, low = above[planes + q], strip_above[q, strip_rows, :]
                inside = slab < slabs - 1
            top, low = top / own, low / rim
            if inside is not None:
                top, low = jnp.where(inside, top, 0.0), jnp.where(inside, low, 0.0)
            ratio[p, 0:rows, :] = top
            ratio[p, rows:used, :] = low

    for p in range(planes):
        for first in range(0, used, 8):
            flat2[p * pitch + first : p * pitch + first + 8, :] = blur_z(
                lambda t: ratio[p + t, first : first + 8, :], [taps_z[t, 0:8, :] for t in range(5)], lanes
            )
        flat2[p * pitch + used : (p + 1) * pitch, :] = jnp.zeros((pitch - used, lanes), F32)
    for start in range(0, planes, 3):
        count = min(3, planes - start)
        back = blur_yx(flat2, start, count, wy2_h, wy2_l)
        for p in range(start, start + count):
            out[p] = back[(p - start) * pitch : (p - start) * pitch + used, :]


def field_kernel(views, rows, place, parts, est, strip, out):
    view, row = place[0], place[2]
    total = parts[0]
    for v in range(1, views):
        total = total + parts[v]
    total = total * (1.0 / views)
    own, rim = est[view], strip[view, 0:EST_STRIP, :]

    @pl.when(row == 0)
    def _():
        value = jnp.concatenate([own * total[0:rows], rim[0:DATA_STRIP] * total[rows:]], axis=0)
        for v in range(views):
            out[v] = value

    @pl.when(row == 1)
    def _():
        value = jnp.concatenate(
            [rim[DATA_STRIP:] * total[0:DATA_STRIP], own * total[DATA_STRIP:]], axis=0
        )
        for v in range(views):
            out[v] = value


def variation_kernel(slabs, rows, place, field, below, above, out, first, second):
    planes, used, lanes = field.shape
    slab, row = place[1], place[2]
    lane = lax.broadcasted_iota(jnp.int32, (used, lanes), 1)
    line = lax.broadcasted_iota(jnp.int32, (used, lanes), 0)

    def up(x, axis, index, last):
        return jnp.where(index == last, 0.0, pltpu.roll(x, x.shape[axis] - 1, axis))

    def down(x, axis, index):
        return jnp.where(index == 0, 0.0, pltpu.roll(x, 1, axis))

    def one_pass(read, low, high, write):
        before = None
        current = read(low - 1)
        for z in range(low - 1, high):
            after = read(z + 1)
            g_z = after - current
            g_y = up(current, 0, line, used - 1) - current
            g_x = up(current, 1, lane, lanes - 1) - current
            scale = lax.rsqrt(g_z * g_z + g_y * g_y + g_x * g_x + EPS2)
            if z < 0:
                scale = jnp.where(slab > 0, scale, 0.0)
            f_z = g_z * scale
            if z >= low:
                f_y, f_x = g_y * scale, g_x * scale
                spread = f_z - before + f_y - down(f_y, 0, line) + f_x - down(f_x, 1, lane)
                value = current + TAU * spread
                if z < 0:
                    value = jnp.where(slab > 0, value, 0.0)
                if z >= planes:
                    value = jnp.where(slab < slabs - 1, value, 0.0)
                write(z, value)
            before, current = f_z, after

    def read_field(z):
        if z < 0:
            return below[z + TV_HALO]
        if z >= planes:
            return above[z - planes]
        return field[z]

    def into(ref):
        def write(z, value):
            ref[z + TV_HALO] = value

        return write

    def last(z, value):
        @pl.when(row == 0)
        def _():
            out[z] = value[0:rows]

        @pl.when(row == 1)
        def _():
            out[z] = value[used - rows :]

    one_pass(read_field, -2, planes + 2, into(first))
    one_pass(lambda z: first[z + TV_HALO], -1, planes + 1, into(second))
    one_pass(lambda z: second[z + TV_HALO], 0, planes, last)


def call(kernel, shapes, scratch, *args):
    specs = [SMEM if jnp.ndim(a) == 1 else VMEM for a in args]
    return pl.pallas_call(
        kernel,
        out_shape=shapes,
        in_specs=specs,
        out_specs=jax.tree.map(lambda _: VMEM, shapes),
        scratch_shapes=scratch,
        compiler_params=pltpu.CompilerParams(vmem_limit_bytes=40 * 2**20),
    )(*args)


def body(data, estimate, profile, band, axes_perm):
    data = data[0]
    planes, rows, lanes = estimate.shape
    views, slabs = lax.axis_size("view"), lax.axis_size("slab")
    view, slab, row = lax.axis_index("view"), lax.axis_index("slab"), lax.axis_index("row")
    place = jnp.stack([view, slab, row]).astype(jnp.int32)
    shape = functools.partial(jax.ShapeDtypeStruct, dtype=F32)
    half = functools.partial(jax.ShapeDtypeStruct, dtype=BF16)
    up = [(i, i + 1) for i in range(slabs - 1)]
    down = [(i + 1, i) for i in range(slabs - 1)]

    start_e = jnp.where(row == 0, rows - EST_STRIP, 0)
    start_d = jnp.where(row == 0, rows - DATA_STRIP, 0)
    edge = jnp.concatenate(
        [
            lax.dynamic_slice_in_dim(estimate, start_e, EST_STRIP, 1),
            lax.dynamic_slice_in_dim(data, start_d, DATA_STRIP, 1),
        ],
        axis=1,
    )
    strip = lax.ppermute(edge, "row", [(0, 1), (1, 0)])
    below = lax.ppermute(jnp.concatenate([estimate, data[planes - WIDTH :]], axis=0), "slab", up)
    above = lax.ppermute(jnp.concatenate([estimate, data[:WIDTH]], axis=0), "slab", down)
    strip_below = lax.ppermute(strip, "slab", up)
    strip_above = lax.ppermute(strip, "slab", down)

    pitch, used = rows + EST_STRIP, rows + DATA_STRIP
    matrices = call(
        functools.partial(weights_kernel, rows),
        [shape((WIDTH + 1, 16, lanes))]
        + [half((lanes, lanes))] * 2
        + [half((3 * pitch, 3 * pitch))] * 4,
        [],
        place, band[0], axes_perm[0], profile.reshape(-1),
    )
    back = call(
        functools.partial(views_kernel, slabs),
        shape((planes, used, lanes)),
        [
            pltpu.VMEM(((planes + 2 * WIDTH) * pitch, lanes), F32),
            pltpu.VMEM((planes + 2 * WIDTH, used, lanes), F32),
            pltpu.VMEM((planes * pitch, lanes), F32),
        ],
        place, estimate, data, strip, below, above, strip_below, strip_above, *matrices,
    )
    parts = lax.all_to_all(back, "view", 0, 0, tiled=True)
    copies = call(
        functools.partial(field_kernel, views, rows),
        shape((views, used, lanes)),
        [],
        place, parts, estimate, strip,
    )
    field = lax.all_to_all(copies, "view", 0, 0, tiled=True)
    field_below = lax.ppermute(field[planes - TV_HALO :], "slab", up)
    field_above = lax.ppermute(field[:TV_HALO], "slab", down)
    deep = pltpu.VMEM((planes + 2 * TV_HALO, used, lanes), F32)
    return call(
        functools.partial(variation_kernel, slabs, rows),
        shape((planes, rows, lanes)),
        [deep, deep],
        place, field, field_below, field_above,
    )


def solution(mesh):
    placed = (
        P("view", "slab", "row", None),
        P("slab", "row", None),
        P("view", None, None),
        P("view", None),
        P("view", None),
    )
    return jax.shard_map(
        body, mesh=mesh, in_specs=placed, out_specs=P("slab", "row", None), check_vma=False
    )
```

```python
import functools

import jax
import jax.numpy as jnp
from jax import lax
from jax.experimental import pallas as pl
from jax.experimental.pallas import tpu as pltpu
from jax.sharding import PartitionSpec as P

PASSES = 3
TAU = 0.05
EPS2 = 0.25
WIDTH = 4
EST_STRIP = 16
DATA_STRIP = 8
TV_HALO = 3
COST = 20000000000
VMEM = pl.BlockSpec(memory_space=pltpu.VMEM)
SMEM = pl.BlockSpec(memory_space=pltpu.SMEM)
F32 = jnp.float32
BF16 = jnp.bfloat16


def split(x):
    high = x.astype(BF16)
    return high, (x - high.astype(F32)).astype(BF16)


def dot3(a_high, a_low, b_high, b_low):
    dot = functools.partial(jnp.dot, preferred_element_type=F32)
    return dot(a_high, b_high) + (dot(a_low, b_high) + dot(a_high, b_low))


def weights_kernel(rows, place, band, perm, prof, taps_z, wx_h, wx_l, wy1_h, wy1_l, wy2_h, wy2_l):
    row = place[2]
    pitch = wy1_h.shape[0] // 3
    halo1, halo2 = pitch - rows, pitch - rows - DATA_STRIP

    def taps(axis, shape):
        k = perm[axis]
        reach = band[k]
        parts = [jnp.where(t <= reach, prof[k * (WIDTH + 1) + t], 0.0) for t in range(WIDTH + 1)]
        total = parts[0]
        for part in parts[1:]:
            total = total + 2.0 * part
        return [jnp.full(shape, part, F32) / jnp.full(shape, total, F32) for part in parts]

    def banded(axis, shape, distance, keep, high, low):
        small = (8, shape[1])
        for start in range(0, shape[0], 16):
            pieces = []
            for t, tap in enumerate(taps(axis, small)):
                pieces.append(jnp.concatenate([tap, tap], axis=0))
            i = start + lax.broadcasted_iota(jnp.int32, (16, shape[1]), 0)
            j = lax.broadcasted_iota(jnp.int32, (16, shape[1]), 1)
            d = jnp.abs(distance(i, j))
            value = jnp.zeros((16, shape[1]), F32)
            for t in range(WIDTH + 1):
                value = jnp.where((d == t) & keep(i, j), pieces[t], value)
            high[start : start + 16, :], low[start : start + 16, :] = split(value)

    for t, tap in enumerate(taps(0, taps_z.shape[1:])):
        taps_z[t] = tap
    banded(2, wx_h.shape, lambda i, j: i - j, lambda i, j: (i >= 0), wx_h, wx_l)

    def plane_of(i):
        return (i >= pitch).astype(jnp.int32) + (i >= 2 * pitch).astype(jnp.int32)

    def halo_place(i, strip):
        i = i - pitch * plane_of(i)
        return jnp.where((i >= rows) & (row == 1), i - rows - strip, i)

    def ascending(i):
        return i - pitch * plane_of(i) - DATA_STRIP * row

    def same(i, j):
        return plane_of(i) == plane_of(j)

    def used(i):
        return i - pitch * plane_of(i) < rows + DATA_STRIP

    banded(
        1,
        wy1_h.shape,
        lambda i, j: halo_place(i, DATA_STRIP) - halo_place(j, EST_STRIP),
        lambda i, j: same(i, j) & used(i),
        wy1_h,
        wy1_l,
    )
    banded(
        1,
        wy2_h.shape,
        lambda i, j: ascending(i) - halo_place(j, DATA_STRIP),
        lambda i, j: same(i, j) & used(i) & used(j),
        wy2_h,
        wy2_l,
    )


def blur_z(read, taps_z):
    total = taps_z[0] * read(WIDTH)
    for t in range(1, WIDTH + 1):
        total = total + taps_z[t] * (read(WIDTH - t) + read(WIDTH + t))
    return total


def views_kernel(
    slabs, place, est, data, strip, est_on, est_off, on, off,
    taps_z, wx_h, wx_l, wy1_h, wy1_l, wy2_h, wy2_l, out, flat1, ratio, flat2,
):
    planes, rows, lanes = est.shape
    slab = place[1]
    pitch = rows + EST_STRIP
    used = rows + DATA_STRIP
    wide = planes + 2 * WIDTH

    odd = lax.rem(slab, 2) == 1

    thick = EST_STRIP + DATA_STRIP
    base = planes * thick

    def blur_first(below, above, strip_below, strip_above):
        def est_plane(q, first):
            ref = (below, est, above)[q // planes]
            return ref[q % planes, first : first + 16, :]

        def est_strip(q):
            if q // planes == 1:
                return strip[q - planes, 0:EST_STRIP, :]
            at = q % planes * thick
            return (strip_below, strip_above)[q // planes // 2][at : at + EST_STRIP, :]

        for p in range(wide):
            for first in range(0, rows, 16):
                flat1[p * pitch + first : p * pitch + first + 16, :] = blur_z(
                    lambda t: est_plane(p + t, first), taps_z
                )
            flat1[p * pitch + rows : (p + 1) * pitch, :] = blur_z(lambda t: est_strip(p + t), taps_z)

    @pl.when(odd)
    def _():
        blur_first(est_on, est_off, on, off)

    @pl.when(jnp.logical_not(odd))
    def _():
        blur_first(est_off, est_on, off, on)

    def blur_yx(flat, start, count, w_h, w_l):
        n = count * pitch
        x_h, x_l = split(flat[start * pitch : start * pitch + n, :])
        mid = dot3(w_h[0:n, 0:n], w_l[0:n, 0:n], x_h, x_l)
        m_h, m_l = split(mid)
        return dot3(m_h, m_l, wx_h[...], wx_l[...])

    for start in range(0, wide, 3):
        count = min(3, wide - start)
        blurred = blur_yx(flat1, start, count, wy1_h, wy1_l)
        for p in range(start, start + count):
            own = blurred[(p - start) * pitch : (p - start) * pitch + rows, :]
            rim = blurred[(p - start) * pitch + rows : (p - start) * pitch + used, :]
            strip_rows = slice(EST_STRIP, EST_STRIP + DATA_STRIP)
            if p < WIDTH:
                top = slice(base + p * rows, base + (p + 1) * rows)
                low = (planes - WIDTH + p) * thick + EST_STRIP
                low = slice(low, low + DATA_STRIP)
                top = jnp.where(odd, on[top, :], off[top, :])
                low = jnp.where(odd, on[low, :], off[low, :])
                inside = slab > 0
            elif p < WIDTH + planes:
                top, low = data[p - WIDTH], strip[p - WIDTH, strip_rows, :]
                inside = None
            else:
                q = p - WIDTH - planes
                top = slice(base + q * rows, base + (q + 1) * rows)
                low = slice(q * thick + EST_STRIP, (q + 1) * thick)
                top = jnp.where(odd, off[top, :], on[top, :])
                low = jnp.where(odd, off[low, :], on[low, :])
                inside = slab < slabs - 1
            top, low = top / own, low / rim
            if inside is not None:
                top, low = jnp.where(inside, top, 0.0), jnp.where(inside, low, 0.0)
            ratio[p, 0:rows, :] = top
            ratio[p, rows:used, :] = low

    for p in range(planes):
        for first in range(0, used, 8):
            flat2[p * pitch + first : p * pitch + first + 8, :] = blur_z(
                lambda t: ratio[p + t, first : first + 8, :], [taps_z[t, 0:8, :] for t in range(5)]
            )
        flat2[p * pitch + used : (p + 1) * pitch, :] = jnp.zeros((pitch - used, lanes), F32)
    for start in range(0, planes, 3):
        count = min(3, planes - start)
        back = blur_yx(flat2, start, count, wy2_h, wy2_l)
        for p in range(start, start + count):
            out[p] = back[(p - start) * pitch : (p - start) * pitch + used, :]


def field_kernel(views, rows, place, parts, est, strip, out):
    view, row = place[0], place[2]
    total = parts[0]
    for v in range(1, views):
        total = total + parts[v]
    total = total * (1.0 / views)
    own, rim = est[view], strip[view, 0:EST_STRIP, :]

    @pl.when(row == 0)
    def _():
        value = jnp.concatenate([own * total[0:rows], rim[0:DATA_STRIP] * total[rows:]], axis=0)
        for v in range(views):
            out[v] = value

    @pl.when(row == 1)
    def _():
        value = jnp.concatenate(
            [rim[DATA_STRIP:] * total[0:DATA_STRIP], own * total[DATA_STRIP:]], axis=0
        )
        for v in range(views):
            out[v] = value


def variation_kernel(slabs, rows, place, field, on, off, out, rims, first, second):
    planes, used, lanes = field.shape
    slab, row = place[1], place[2]
    lane = lax.broadcasted_iota(jnp.int32, (used, lanes), 1)
    line = lax.broadcasted_iota(jnp.int32, (used, lanes), 0)

    odd = lax.rem(slab, 2)
    rims[pl.ds(odd * TV_HALO, TV_HALO)] = off[...]
    rims[pl.ds((1 - odd) * TV_HALO, TV_HALO)] = on[...]

    def up(x, axis, index, last):
        return jnp.where(index == last, 0.0, pltpu.roll(x, x.shape[axis] - 1, axis))

    def down(x, axis, index):
        return jnp.where(index == 0, 0.0, pltpu.roll(x, 1, axis))

    def one_pass(read, low, high, write):
        before = None
        current = read(low - 1)
        for z in range(low - 1, high):
            after = read(z + 1)
            g_z = after - current
            g_y = up(current, 0, line, used - 1) - current
            g_x = up(current, 1, lane, lanes - 1) - current
            scale = lax.rsqrt(g_z * g_z + g_y * g_y + g_x * g_x + EPS2)
            if z < 0:
                scale = jnp.where(slab > 0, scale, 0.0)
            f_z = g_z * scale
            if z >= low:
                f_y, f_x = g_y * scale, g_x * scale
                spread = f_z - before + f_y - down(f_y, 0, line) + f_x - down(f_x, 1, lane)
                value = current + TAU * spread
                if z < 0:
                    value = jnp.where(slab > 0, value, 0.0)
                if z >= planes:
                    value = jnp.where(slab < slabs - 1, value, 0.0)
                write(z, value)
            before, current = f_z, after

    def read_field(z):
        if z < 0:
            return rims[z + TV_HALO]
        if z >= planes:
            return rims[z - planes + TV_HALO]
        return field[z]

    def into(ref):
        def write(z, value):
            ref[z + TV_HALO] = value

        return write

    def last(z, value):
        @pl.when(row == 0)
        def _():
            out[z] = value[0:rows]

        @pl.when(row == 1)
        def _():
            out[z] = value[used - rows :]

    one_pass(read_field, -2, planes + 2, into(first))
    one_pass(lambda z: first[z + TV_HALO], -1, planes + 1, into(second))
    one_pass(lambda z: second[z + TV_HALO], 0, planes, last)


def call(kernel, shapes, scratch, *args, cost=None):
    specs = [SMEM if jnp.ndim(a) == 1 else VMEM for a in args]
    return pl.pallas_call(
        kernel,
        out_shape=shapes,
        in_specs=specs,
        out_specs=jax.tree.map(lambda _: VMEM, shapes),
        scratch_shapes=scratch,
        cost_estimate=cost,
        compiler_params=pltpu.CompilerParams(vmem_limit_bytes=16 * 2**20),
    )(*args)


def body(data, estimate, profile, band, axes_perm):
    data = data[0]
    planes, rows, lanes = estimate.shape
    views, slabs = lax.axis_size("view"), lax.axis_size("slab")
    view, slab, row = lax.axis_index("view"), lax.axis_index("slab"), lax.axis_index("row")
    place = jnp.stack([view, slab, row]).astype(jnp.int32)
    shape = functools.partial(jax.ShapeDtypeStruct, dtype=F32)
    half = functools.partial(jax.ShapeDtypeStruct, dtype=BF16)
    off_pairs = [(i, i + 1) for i in range(1, slabs - 1, 2)]
    off_pairs += [(target, source) for source, target in off_pairs]
    on_pairs = [(i, i ^ 1) for i in range(slabs)]
    odd = lax.rem(slab, 2)

    first_row, is_odd = row == 0, odd == 1
    edge = jnp.concatenate(
        [
            jnp.where(first_row, estimate[:, rows - EST_STRIP :], estimate[:, :EST_STRIP]),
            jnp.where(first_row, data[:, rows - DATA_STRIP :], data[:, :DATA_STRIP]),
        ],
        axis=1,
    )
    strip = lax.ppermute(edge, "row", [(0, 1), (1, 0)])
    held = lax.optimization_barrier((estimate, edge))[0]
    est_off = lax.ppermute(held, "slab", off_pairs)
    est_on = lax.ppermute(held, "slab", on_pairs)
    low = data[:WIDTH].reshape(-1, lanes)
    high = data[planes - WIDTH :].reshape(-1, lanes)
    flat = strip.reshape(-1, lanes)
    off = jnp.concatenate([flat, jnp.where(is_odd, high, low)], axis=0)
    on = jnp.concatenate([flat, jnp.where(is_odd, low, high)], axis=0)
    off = lax.ppermute(off, "slab", off_pairs)
    on = lax.ppermute(on, "slab", on_pairs)

    pitch, used = rows + EST_STRIP, rows + DATA_STRIP
    matrices = call(
        functools.partial(weights_kernel, rows),
        [shape((WIDTH + 1, 16, lanes))]
        + [half((lanes, lanes))] * 2
        + [half((3 * pitch, 3 * pitch))] * 4,
        [],
        place, band[0], axes_perm[0], profile.reshape(-1),
        cost=pl.CostEstimate(flops=COST, bytes_accessed=0, transcendentals=0),
    )
    back = call(
        functools.partial(views_kernel, slabs),
        shape((planes, used, lanes)),
        [
            pltpu.VMEM(((planes + 2 * WIDTH) * pitch, lanes), F32),
            pltpu.VMEM((planes + 2 * WIDTH, used, lanes), F32),
            pltpu.VMEM((planes * pitch, lanes), F32),
        ],
        place, estimate, data, strip, est_on, est_off, on, off, *matrices,
    )
    parts = lax.all_to_all(back, "view", 0, 0, tiled=True)
    copies = call(
        functools.partial(field_kernel, views, rows),
        shape((views, used, lanes)),
        [],
        place, parts, estimate, strip,
    )
    field = lax.all_to_all(copies, "view", 0, 0, tiled=True)
    reach = planes - TV_HALO
    low, high = field[:TV_HALO], field[reach:]
    off = lax.ppermute(jnp.where(is_odd, high, low), "slab", off_pairs)
    on = lax.ppermute(jnp.where(is_odd, low, high), "slab", on_pairs)
    deep = pltpu.VMEM((planes + 2 * TV_HALO, used, lanes), F32)
    return call(
        functools.partial(variation_kernel, slabs, rows),
        shape((planes, rows, lanes)),
        [pltpu.VMEM((2 * TV_HALO, used, lanes), F32), deep, deep],
        place, field, on, off,
    )


def solution(mesh):
    placed = (
        P("view", "slab", "row", None),
        P("slab", "row", None),
        P("view", None, None),
        P("view", None),
        P("view", None),
    )
    return jax.shard_map(
        body, mesh=mesh, in_specs=placed, out_specs=P("slab", "row", None), check_vma=False
    )
```

```python
import functools

import jax
import jax.numpy as jnp
from jax import lax
from jax.experimental import pallas as pl
from jax.experimental.pallas import tpu as pltpu
from jax.sharding import PartitionSpec as P

PASSES = 3
TAU = 0.05
EPS2 = 0.25
WIDTH = 4
EST_STRIP = 16
DATA_STRIP = 8
TV_HALO = 3
COST = 20000000000
VMEM = pl.BlockSpec(memory_space=pltpu.VMEM)
SMEM = pl.BlockSpec(memory_space=pltpu.SMEM)
F32 = jnp.float32
BF16 = jnp.bfloat16


def split(x):
    high = x.astype(BF16)
    return high, (x - high.astype(F32)).astype(BF16)


def dot3(a_high, a_low, b_high, b_low):
    dot = functools.partial(jnp.dot, preferred_element_type=F32)
    return dot(a_high, b_high) + (dot(a_low, b_high) + dot(a_high, b_low))


def weights_kernel(rows, place, band, perm, prof, taps_z, wx_h, wx_l, wy1_h, wy1_l, wy2_h, wy2_l):
    row = place[2]
    pitch = wy1_h.shape[0] // 3
    halo1, halo2 = pitch - rows, pitch - rows - DATA_STRIP

    def taps(axis, shape):
        k = perm[0, axis]
        reach = band[0, k]
        parts = [jnp.where(t <= reach, prof[0, k, t], 0.0) for t in range(WIDTH + 1)]
        total = parts[0]
        for part in parts[1:]:
            total = total + 2.0 * part
        return [jnp.full(shape, part, F32) / jnp.full(shape, total, F32) for part in parts]

    def banded(axis, shape, distance, keep, high, low):
        small = (8, shape[1])
        for start in range(0, shape[0], 16):
            pieces = []
            for t, tap in enumerate(taps(axis, small)):
                pieces.append(jnp.concatenate([tap, tap], axis=0))
            i = start + lax.broadcasted_iota(jnp.int32, (16, shape[1]), 0)
            j = lax.broadcasted_iota(jnp.int32, (16, shape[1]), 1)
            d = jnp.abs(distance(i, j))
            value = jnp.zeros((16, shape[1]), F32)
            for t in range(WIDTH + 1):
                value = jnp.where((d == t) & keep(i, j), pieces[t], value)
            high[start : start + 16, :], low[start : start + 16, :] = split(value)

    for t, tap in enumerate(taps(0, taps_z.shape[1:])):
        taps_z[t] = tap
    banded(2, wx_h.shape, lambda i, j: i - j, lambda i, j: (i >= 0), wx_h, wx_l)

    def plane_of(i):
        return (i >= pitch).astype(jnp.int32) + (i >= 2 * pitch).astype(jnp.int32)

    def halo_place(i, strip):
        i = i - pitch * plane_of(i)
        return jnp.where((i >= rows) & (row == 1), i - rows - strip, i)

    def ascending(i):
        return i - pitch * plane_of(i) - DATA_STRIP * row

    def same(i, j):
        return plane_of(i) == plane_of(j)

    def used(i):
        return i - pitch * plane_of(i) < rows + DATA_STRIP

    banded(
        1,
        wy1_h.shape,
        lambda i, j: halo_place(i, DATA_STRIP) - halo_place(j, EST_STRIP),
        lambda i, j: same(i, j) & used(i),
        wy1_h,
        wy1_l,
    )
    banded(
        1,
        wy2_h.shape,
        lambda i, j: ascending(i) - halo_place(j, DATA_STRIP),
        lambda i, j: same(i, j) & used(i) & used(j),
        wy2_h,
        wy2_l,
    )


def blur_z(read, taps_z):
    total = taps_z[0] * read(WIDTH)
    for t in range(1, WIDTH + 1):
        total = total + taps_z[t] * (read(WIDTH - t) + read(WIDTH + t))
    return total


def views_kernel(
    slabs, place, est, data, strip, est_on, est_off, on, off,
    taps_z, wx_h, wx_l, wy1_h, wy1_l, wy2_h, wy2_l, out, flat1, ratio, flat2,
):
    planes, rows, lanes = est.shape
    slab = place[1]
    pitch = rows + EST_STRIP
    used = rows + DATA_STRIP
    wide = planes + 2 * WIDTH

    odd = lax.rem(slab, 2) == 1

    thick = EST_STRIP + DATA_STRIP
    base = planes * thick

    def blur_first(below, above, strip_below, strip_above):
        def est_plane(q, first):
            ref = (below, est, above)[q // planes]
            return ref[q % planes, first : first + 16, :]

        def est_strip(q):
            if q // planes == 1:
                return strip[q - planes, 0:EST_STRIP, :]
            at = q % planes * thick
            return (strip_below, strip_above)[q // planes // 2][at : at + EST_STRIP, :]

        for p in range(wide):
            for first in range(0, rows, 16):
                flat1[p * pitch + first : p * pitch + first + 16, :] = blur_z(
                    lambda t: est_plane(p + t, first), taps_z
                )
            flat1[p * pitch + rows : (p + 1) * pitch, :] = blur_z(lambda t: est_strip(p + t), taps_z)

    @pl.when(odd)
    def _():
        blur_first(est_on, est_off, on, off)

    @pl.when(jnp.logical_not(odd))
    def _():
        blur_first(est_off, est_on, off, on)

    def blur_yx(flat, start, count, w_h, w_l):
        n = count * pitch
        x_h, x_l = split(flat[start * pitch : start * pitch + n, :])
        mid = dot3(w_h[0:n, 0:n], w_l[0:n, 0:n], x_h, x_l)
        m_h, m_l = split(mid)
        return dot3(m_h, m_l, wx_h[...], wx_l[...])

    for start in range(0, wide, 3):
        count = min(3, wide - start)
        blurred = blur_yx(flat1, start, count, wy1_h, wy1_l)
        for p in range(start, start + count):
            own = blurred[(p - start) * pitch : (p - start) * pitch + rows, :]
            rim = blurred[(p - start) * pitch + rows : (p - start) * pitch + used, :]
            strip_rows = slice(EST_STRIP, EST_STRIP + DATA_STRIP)
            if p < WIDTH:
                top = slice(base + p * rows, base + (p + 1) * rows)
                low = (planes - WIDTH + p) * thick + EST_STRIP
                low = slice(low, low + DATA_STRIP)
                top = jnp.where(odd, on[top, :], off[top, :])
                low = jnp.where(odd, on[low, :], off[low, :])
                inside = slab > 0
            elif p < WIDTH + planes:
                top, low = data[p - WIDTH], strip[p - WIDTH, strip_rows, :]
                inside = None
            else:
                q = p - WIDTH - planes
                top = slice(base + q * rows, base + (q + 1) * rows)
                low = slice(q * thick + EST_STRIP, (q + 1) * thick)
                top = jnp.where(odd, off[top, :], on[top, :])
                low = jnp.where(odd, off[low, :], on[low, :])
                inside = slab < slabs - 1
            top, low = top / own, low / rim
            if inside is not None:
                top, low = jnp.where(inside, top, 0.0), jnp.where(inside, low, 0.0)
            ratio[p, 0:rows, :] = top
            ratio[p, rows:used, :] = low

    for p in range(planes):
        for first in range(0, used, 8):
            flat2[p * pitch + first : p * pitch + first + 8, :] = blur_z(
                lambda t: ratio[p + t, first : first + 8, :], [taps_z[t, 0:8, :] for t in range(5)]
            )
        flat2[p * pitch + used : (p + 1) * pitch, :] = jnp.zeros((pitch - used, lanes), F32)
    for start in range(0, planes, 3):
        count = min(3, planes - start)
        back = blur_yx(flat2, start, count, wy2_h, wy2_l)
        for p in range(start, start + count):
            out[p] = back[(p - start) * pitch : (p - start) * pitch + used, :]


def field_kernel(views, rows, place, parts, est, strip, out):
    view, row = place[0], place[2]
    total = parts[0]
    for v in range(1, views):
        total = total + parts[v]
    total = total * (1.0 / views)
    own, rim = est[view], strip[view, 0:EST_STRIP, :]

    @pl.when(row == 0)
    def _():
        value = jnp.concatenate([own * total[0:rows], rim[0:DATA_STRIP] * total[rows:]], axis=0)
        for v in range(views):
            out[v] = value

    @pl.when(row == 1)
    def _():
        value = jnp.concatenate(
            [rim[DATA_STRIP:] * total[0:DATA_STRIP], own * total[DATA_STRIP:]], axis=0
        )
        for v in range(views):
            out[v] = value


def variation_kernel(slabs, rows, place, field, on, off, out, start, first, second):
    planes, used, lanes = field.shape
    slab, row = place[1], place[2]
    half = lanes // 2
    odd = lax.rem(slab, 2)
    start[pl.ds(odd * (planes + TV_HALO), TV_HALO)] = off[...]
    start[pl.ds((1 - odd) * (planes + TV_HALO), TV_HALO)] = on[...]
    start[TV_HALO : TV_HALO + planes] = field[...]
    lane = lax.broadcasted_iota(jnp.int32, (1, 1, half), 2)
    line = lax.broadcasted_iota(jnp.int32, (1, 8, half), 1)

    def next_x(x):
        turned = [pltpu.roll(h, half - 1, 2) for h in x]
        return [
            jnp.where(lane == half - 1, turned[1], turned[0]),
            jnp.where(lane == half - 1, 0.0, turned[1]),
        ]

    def last_x(x):
        turned = [pltpu.roll(h, 1, 2) for h in x]
        return [jnp.where(lane == 0, 0.0, turned[0]), jnp.where(lane == 0, turned[0], turned[1])]

    def next_y(x):
        turned = pltpu.roll(x, used - 1, 1)
        last = jnp.where(line == 7, 0.0, turned[:, used - 8 :])
        return jnp.concatenate([turned[:, : used - 8], last], axis=1)

    def last_y(x):
        turned = pltpu.roll(x, 1, 1)
        return jnp.concatenate([jnp.where(line == 0, 0.0, turned[:, :8]), turned[:, 8:]], axis=1)

    def masked(x, z):
        if z >= TV_HALO and z + x.shape[0] <= TV_HALO + planes:
            return x
        parts = []
        for i in range(x.shape[0]):
            part = x[i : i + 1]
            if z + i < TV_HALO:
                part = jnp.where(slab > 0, part, 0.0)
            elif z + i >= TV_HALO + planes:
                part = jnp.where(slab < slabs - 1, part, 0.0)
            parts.append(part)
        return jnp.concatenate(parts, axis=0) if len(parts) > 1 else parts[0]

    def flux(source, z, count, only_z):
        box = [slice(h * half, (h + 1) * half) for h in range(2)]
        now = [source[z : z + count, :, b] for b in box]
        after = [source[z + 1 : z + count + 1, :, b] for b in box]
        side = next_x(now)
        f_x, f_y, f_z = [], [], []
        for h in range(2):
            g_z, g_y, g_x = after[h] - now[h], next_y(now[h]) - now[h], side[h] - now[h]
            scale = masked(lax.rsqrt(g_z * g_z + g_y * g_y + g_x * g_x + EPS2), z)
            f_z.append(g_z * scale)
            if not only_z:
                f_y.append(g_y * scale)
                f_x.append(g_x * scale)
        return now, f_x, f_y, f_z

    def one_pass(source, low, high, group, target):
        before = flux(source, low - 1, 1, True)[3]
        for z in range(low, high, group):
            count = min(group, high - z)
            now, f_x, f_y, f_z = flux(source, z, count, False)
            side = last_x(f_x)
            for h in range(2):
                below = before[h]
                if count > 1:
                    below = jnp.concatenate([below, f_z[h][: count - 1]], axis=0)
                spread = (f_z[h] - below) + (f_y[h] - last_y(f_y[h])) + (f_x[h] - side[h])
                target[z : z + count, :, h * half : (h + 1) * half] = masked(now[h] + TAU * spread, z)
            before = [f[count - 1 : count] for f in f_z]

    deep = planes + 2 * TV_HALO
    groups = (4, 5, 4)
    one_pass(start, 1, deep - 1, groups[0], first)
    one_pass(first, 2, deep - 2, groups[1], second)
    one_pass(second, 3, deep - 3, groups[2], first)
    skip = pl.multiple_of(row * (used - rows), 8)
    out[...] = first[TV_HALO : TV_HALO + planes, pl.ds(skip, rows), :]


def call(kernel, shapes, scratch, *args, cost=None, scalars=1):
    specs = [SMEM if i < scalars else VMEM for i in range(len(args))]
    return pl.pallas_call(
        kernel,
        out_shape=shapes,
        in_specs=specs,
        out_specs=jax.tree.map(lambda _: VMEM, shapes),
        scratch_shapes=scratch,
        cost_estimate=cost,
        compiler_params=pltpu.CompilerParams(vmem_limit_bytes=16 * 2**20),
    )(*args)


def body(data, estimate, profile, band, axes_perm):
    data = data[0]
    planes, rows, lanes = estimate.shape
    views, slabs = lax.axis_size("view"), lax.axis_size("slab")
    view, slab, row = lax.axis_index("view"), lax.axis_index("slab"), lax.axis_index("row")
    place = jnp.stack([view, slab, row]).astype(jnp.int32)
    shape = functools.partial(jax.ShapeDtypeStruct, dtype=F32)
    half = functools.partial(jax.ShapeDtypeStruct, dtype=BF16)
    off_pairs = [(i, i + 1) for i in range(1, slabs - 1, 2)]
    off_pairs += [(target, source) for source, target in off_pairs]
    on_pairs = [(i, i ^ 1) for i in range(slabs)]
    odd = lax.rem(slab, 2)

    first_row, is_odd = row == 0, odd == 1
    edge = jnp.concatenate(
        [
            jnp.where(first_row, estimate[:, rows - EST_STRIP :], estimate[:, :EST_STRIP]),
            jnp.where(first_row, data[:, rows - DATA_STRIP :], data[:, :DATA_STRIP]),
        ],
        axis=1,
    )
    strip = lax.ppermute(edge, "row", [(0, 1), (1, 0)])
    held = lax.optimization_barrier((estimate, edge))[0]
    est_off = lax.ppermute(held, "slab", off_pairs)
    est_on = lax.ppermute(held, "slab", on_pairs)
    low = data[:WIDTH].reshape(-1, lanes)
    high = data[planes - WIDTH :].reshape(-1, lanes)
    flat = strip.reshape(-1, lanes)
    off = jnp.concatenate([flat, jnp.where(is_odd, high, low)], axis=0)
    on = jnp.concatenate([flat, jnp.where(is_odd, low, high)], axis=0)
    off = lax.ppermute(off, "slab", off_pairs)
    on = lax.ppermute(on, "slab", on_pairs)

    pitch, used = rows + EST_STRIP, rows + DATA_STRIP
    matrices = call(
        functools.partial(weights_kernel, rows),
        [shape((WIDTH + 1, 16, lanes))]
        + [half((lanes, lanes))] * 2
        + [half((3 * pitch, 3 * pitch))] * 4,
        [],
        place, band, axes_perm, profile,
        scalars=4,
        cost=pl.CostEstimate(flops=COST, bytes_accessed=0, transcendentals=0),
    )
    back = call(
        functools.partial(views_kernel, slabs),
        shape((planes, used, lanes)),
        [
            pltpu.VMEM(((planes + 2 * WIDTH) * pitch, lanes), F32),
            pltpu.VMEM((planes + 2 * WIDTH, used, lanes), F32),
            pltpu.VMEM((planes * pitch, lanes), F32),
        ],
        place, estimate, data, strip, est_on, est_off, on, off, *matrices,
    )
    parts = lax.all_to_all(back, "view", 0, 0, tiled=True)
    copies = call(
        functools.partial(field_kernel, views, rows),
        shape((views, used, lanes)),
        [],
        place, parts, estimate, strip,
    )
    field = lax.all_to_all(copies, "view", 0, 0, tiled=True)
    reach = planes - TV_HALO
    low, high = field[:TV_HALO], field[reach:]
    off = lax.ppermute(jnp.where(is_odd, high, low), "slab", off_pairs)
    on = lax.ppermute(jnp.where(is_odd, low, high), "slab", on_pairs)
    deep = pltpu.VMEM((planes + 2 * TV_HALO, used, lanes), F32)
    return call(
        functools.partial(variation_kernel, slabs, rows),
        shape((planes, rows, lanes)),
        [deep, deep, deep],
        place, field, on, off,
    )


def solution(mesh):
    placed = (
        P("view", "slab", "row", None),
        P("slab", "row", None),
        P("view", None, None),
        P("view", None),
        P("view", None),
    )
    return jax.shard_map(
        body, mesh=mesh, in_specs=placed, out_specs=P("slab", "row", None), check_vma=False
    )
```

```python
import functools

import jax
import jax.numpy as jnp
from jax import lax
from jax.experimental import pallas as pl
from jax.experimental.pallas import tpu as pltpu
from jax.sharding import PartitionSpec as P

PASSES = 3
TAU = 0.05
EPS2 = 0.25
WIDTH = 4
EST_STRIP = 16
DATA_STRIP = 8
TV_HALO = 3
COST = 20000000000
VMEM = pl.BlockSpec(memory_space=pltpu.VMEM)
SMEM = pl.BlockSpec(memory_space=pltpu.SMEM)
F32 = jnp.float32
BF16 = jnp.bfloat16


def split(x):
    high = x.astype(BF16)
    return high, (x - high.astype(F32)).astype(BF16)


def dot3(a_high, a_low, b_high, b_low):
    dot = functools.partial(jnp.dot, preferred_element_type=F32)
    return dot(a_high, b_high) + (dot(a_low, b_high) + dot(a_high, b_low))


def weights_kernel(rows, place, band, perm, prof, taps_z, wx_h, wx_l, wo_h, wo_l, wr_h, wr_l, wy2_h, wy2_l):
    row = place[2]
    pitch = wy2_h.shape[0] // 3
    used = rows + DATA_STRIP

    def taps(axis, shape):
        k = perm[0, axis]
        reach = band[0, k]
        parts = [jnp.where(t <= reach, prof[0, k, t], 0.0) for t in range(WIDTH + 1)]
        total = parts[0]
        for part in parts[1:]:
            total = total + 2.0 * part
        return [jnp.full(shape, part, F32) / jnp.full(shape, total, F32) for part in parts]

    def banded(axis, shape, distance, keep, high, low):
        small = (8, shape[1])
        for start in range(0, shape[0], 16):
            pieces = []
            for t, tap in enumerate(taps(axis, small)):
                pieces.append(jnp.concatenate([tap, tap], axis=0))
            i = start + lax.broadcasted_iota(jnp.int32, (16, shape[1]), 0)
            j = lax.broadcasted_iota(jnp.int32, (16, shape[1]), 1)
            d = jnp.abs(distance(i, j))
            value = jnp.zeros((16, shape[1]), F32)
            for t in range(WIDTH + 1):
                value = jnp.where((d == t) & keep(i, j), pieces[t], value)
            high[start : start + 16, :], low[start : start + 16, :] = split(value)

    for t, tap in enumerate(taps(0, taps_z.shape[1:])):
        taps_z[t] = tap
    banded(2, wx_h.shape, lambda i, j: i - j, lambda i, j: (i >= 0), wx_h, wx_l)

    most = wo_h.shape[0]

    def plane_of(i, height):
        return sum((i >= n * height).astype(jnp.int32) for n in range(1, most // height))

    def within(i, height):
        return i - height * plane_of(i, height)

    def halo_place(i, strip):
        return jnp.where((i >= rows) & (row == 1), i - rows - strip, i)

    def reached(i):
        return jnp.where(i < 8, i + (rows - 8) * (1 - row), halo_place(i - 8 + rows, DATA_STRIP))

    def ascending(i):
        return within(i, pitch) - DATA_STRIP * row

    banded(
        1,
        wo_h.shape,
        lambda i, j: halo_place(within(i, used), DATA_STRIP) - within(j, rows),
        lambda i, j: plane_of(i, used) == plane_of(j, rows),
        wo_h,
        wo_l,
    )
    banded(
        1,
        wr_h.shape,
        lambda i, j: reached(within(i, 16)) - halo_place(within(j, 16) + rows, EST_STRIP),
        lambda i, j: plane_of(i, 16) == plane_of(j, 16),
        wr_h,
        wr_l,
    )
    banded(
        1,
        wy2_h.shape,
        lambda i, j: ascending(i) - halo_place(within(j, pitch), DATA_STRIP),
        lambda i, j: (plane_of(i, pitch) == plane_of(j, pitch))
        & (within(i, pitch) < used)
        & (within(j, pitch) < used),
        wy2_h,
        wy2_l,
    )


def blur_z(read, taps_z):
    taps = [taps_z[t, 0:1, :] for t in range(WIDTH + 1)]
    total = taps[0] * read(WIDTH)
    for t in range(1, WIDTH + 1):
        total = total + taps[t] * (read(WIDTH - t) + read(WIDTH + t))
    return total


def blur_yx(x, w_h, w_l, wx_h, wx_l):
    x_h, x_l = split(x)
    m_h, m_l = split(dot3(w_h, w_l, x_h, x_l))
    return dot3(m_h, m_l, wx_h[...], wx_l[...])


def own_kernel(place, est, est_off, est_on, taps_z, wx_h, wx_l, wo_h, wo_l, out, flat):
    planes, rows, lanes = est.shape
    wide, used, _ = out.shape
    odd = lax.rem(place[1], 2) == 1
    group = 256 // rows

    def blur_first(below, above):
        for p in range(wide):
            flat[p * rows : (p + 1) * rows, :] = blur_z(
                lambda t: (below, est, above)[(p + t) // planes][(p + t) % planes], taps_z
            )

    @pl.when(odd)
    def _():
        blur_first(est_on, est_off)

    @pl.when(jnp.logical_not(odd))
    def _():
        blur_first(est_off, est_on)

    for p in range(0, wide, group):
        part = flat[p * rows : (p + group) * rows, :]
        part = blur_yx(part, wo_h[...], wo_l[...], wx_h, wx_l)
        out[p : p + group] = part.reshape(group, used, lanes)


def views_kernel(
    slabs, place, partial, data, strip, off, on,
    taps_z, wx_h, wx_l, wr_h, wr_l, wy2_h, wy2_l, out, rims, ratio, flat,
):
    planes, rows, lanes = data.shape
    slab, row = place[1], place[2]
    pitch = rows + EST_STRIP
    used = rows + DATA_STRIP
    wide = planes + 2 * WIDTH
    thick = EST_STRIP + DATA_STRIP
    base = planes * thick
    odd = lax.rem(slab, 2) == 1

    def blur_first(below, above):
        def read(q):
            if q // planes == 1:
                return strip[q - planes, 0:EST_STRIP, :]
            at = q % planes * thick
            return (below, above)[q // planes // 2][at : at + EST_STRIP, :]

        for p in range(wide):
            rims[p * EST_STRIP : (p + 1) * EST_STRIP, :] = blur_z(lambda t: read(p + t), taps_z)

    @pl.when(odd)
    def _():
        blur_first(on, off)

    @pl.when(jnp.logical_not(odd))
    def _():
        blur_first(off, on)

    reached = blur_yx(rims[...], wr_h[...], wr_l[...], wx_h, wx_l).reshape(wide, 16, lanes)

    for p in range(wide):
        near, far = reached[p, 0:8], reached[p, 8:16]
        blurred = jnp.concatenate(
            [
                partial[p, 0:8, :] + jnp.where(row == 1, near, 0.0),
                partial[p, 8 : rows - 8, :],
                partial[p, rows - 8 : rows, :] + jnp.where(row == 0, near, 0.0),
                partial[p, rows:used, :] + far,
            ],
            axis=0,
        )
        if WIDTH <= p < WIDTH + planes:
            top, low = data[p - WIDTH], strip[p - WIDTH, EST_STRIP:thick, :]
        else:
            lower = p < WIDTH
            first, second = (on, off) if lower else (off, on)
            q = p if lower else p - WIDTH - planes
            top = slice(base + q * rows, base + (q + 1) * rows)
            low = (q + planes - WIDTH if lower else q) * thick + EST_STRIP
            low = slice(low, low + DATA_STRIP)
            top = jnp.where(odd, first[top, :], second[top, :])
            low = jnp.where(odd, first[low, :], second[low, :])
        value = jnp.concatenate([top, low], axis=0) / blurred
        if p < WIDTH:
            value = jnp.where(slab > 0, value, 0.0)
        if p >= WIDTH + planes:
            value = jnp.where(slab < slabs - 1, value, 0.0)
        ratio[p] = value

    for p in range(planes):
        flat[p * pitch : p * pitch + used, :] = blur_z(lambda t: ratio[p + t], taps_z)
        flat[p * pitch + used : (p + 1) * pitch, :] = jnp.zeros((pitch - used, lanes), F32)
    for start in range(0, planes, 3):
        count = min(3, planes - start)
        n = count * pitch
        part = flat[start * pitch : start * pitch + n, :]
        part = blur_yx(part, wy2_h[0:n, 0:n], wy2_l[0:n, 0:n], wx_h, wx_l)
        out[start : start + count] = part.reshape(count, pitch, lanes)[:, :used]


def field_kernel(views, rows, place, parts, est, strip, out):
    view, row = place[0], place[2]
    total = parts[0]
    for v in range(1, views):
        total = total + parts[v]
    total = total * (1.0 / views)
    own, rim = est[view], strip[view, 0:EST_STRIP, :]

    @pl.when(row == 0)
    def _():
        value = jnp.concatenate([own * total[0:rows], rim[0:DATA_STRIP] * total[rows:]], axis=0)
        for v in range(views):
            out[v] = value

    @pl.when(row == 1)
    def _():
        value = jnp.concatenate(
            [rim[DATA_STRIP:] * total[0:DATA_STRIP], own * total[DATA_STRIP:]], axis=0
        )
        for v in range(views):
            out[v] = value


def variation_kernel(slabs, rows, place, field, off, on, out, start, first, second):
    planes, used, lanes = field.shape
    slab, row = place[1], place[2]
    half = lanes // 2
    odd = lax.rem(slab, 2)
    start[pl.ds(odd * (planes + TV_HALO), TV_HALO)] = off[...]
    start[pl.ds((1 - odd) * (planes + TV_HALO), TV_HALO)] = on[...]
    start[TV_HALO : TV_HALO + planes] = field[...]
    lane = lax.broadcasted_iota(jnp.int32, (1, 1, half), 2)
    line = lax.broadcasted_iota(jnp.int32, (1, 8, half), 1)

    def next_x(x):
        turned = [pltpu.roll(h, half - 1, 2) for h in x]
        return [
            jnp.where(lane == half - 1, turned[1], turned[0]),
            jnp.where(lane == half - 1, 0.0, turned[1]),
        ]

    def last_x(x):
        turned = [pltpu.roll(h, 1, 2) for h in x]
        return [jnp.where(lane == 0, 0.0, turned[0]), jnp.where(lane == 0, turned[0], turned[1])]

    def next_y(x):
        turned = pltpu.roll(x, used - 1, 1)
        last = jnp.where(line == 7, 0.0, turned[:, used - 8 :])
        return jnp.concatenate([turned[:, : used - 8], last], axis=1)

    def last_y(x):
        turned = pltpu.roll(x, 1, 1)
        return jnp.concatenate([jnp.where(line == 0, 0.0, turned[:, :8]), turned[:, 8:]], axis=1)

    def masked(x, z):
        if z >= TV_HALO and z + x.shape[0] <= TV_HALO + planes:
            return x
        parts = []
        for i in range(x.shape[0]):
            part = x[i : i + 1]
            if z + i < TV_HALO:
                part = jnp.where(slab > 0, part, 0.0)
            elif z + i >= TV_HALO + planes:
                part = jnp.where(slab < slabs - 1, part, 0.0)
            parts.append(part)
        return jnp.concatenate(parts, axis=0) if len(parts) > 1 else parts[0]

    def flux(source, z, count, only_z):
        box = [slice(h * half, (h + 1) * half) for h in range(2)]
        now = [source[z : z + count, :, b] for b in box]
        after = [source[z + 1 : z + count + 1, :, b] for b in box]
        side = next_x(now)
        f_x, f_y, f_z = [], [], []
        for h in range(2):
            g_z, g_y, g_x = after[h] - now[h], next_y(now[h]) - now[h], side[h] - now[h]
            scale = masked(lax.rsqrt(g_z * g_z + g_y * g_y + g_x * g_x + EPS2), z)
            f_z.append(g_z * scale)
            if not only_z:
                f_y.append(g_y * scale)
                f_x.append(g_x * scale)
        return now, f_x, f_y, f_z

    def one_pass(source, low, high, group, target):
        before = flux(source, low - 1, 1, True)[3]
        for z in range(low, high, group):
            count = min(group, high - z)
            now, f_x, f_y, f_z = flux(source, z, count, False)
            side = last_x(f_x)
            for h in range(2):
                below = before[h]
                if count > 1:
                    below = jnp.concatenate([below, f_z[h][: count - 1]], axis=0)
                spread = (f_z[h] - below) + (f_y[h] - last_y(f_y[h])) + (f_x[h] - side[h])
                target[z : z + count, :, h * half : (h + 1) * half] = masked(now[h] + TAU * spread, z)
            before = [f[count - 1 : count] for f in f_z]

    deep = planes + 2 * TV_HALO
    groups = (4, 5, 4)
    one_pass(start, 1, deep - 1, groups[0], first)
    one_pass(first, 2, deep - 2, groups[1], second)
    one_pass(second, 3, deep - 3, groups[2], first)
    skip = pl.multiple_of(row * (used - rows), 8)
    out[...] = first[TV_HALO : TV_HALO + planes, pl.ds(skip, rows), :]


def call(kernel, shapes, scratch, *args, cost=None, scalars=1):
    specs = [SMEM if i < scalars else VMEM for i in range(len(args))]
    return pl.pallas_call(
        kernel,
        out_shape=shapes,
        in_specs=specs,
        out_specs=jax.tree.map(lambda _: VMEM, shapes),
        scratch_shapes=scratch,
        cost_estimate=cost,
        compiler_params=pltpu.CompilerParams(vmem_limit_bytes=16 * 2**20),
    )(*args)


def body(data, estimate, profile, band, axes_perm):
    data = data[0]
    planes, rows, lanes = estimate.shape
    views, slabs = lax.axis_size("view"), lax.axis_size("slab")
    view, slab, row = lax.axis_index("view"), lax.axis_index("slab"), lax.axis_index("row")
    place = jnp.stack([view, slab, row]).astype(jnp.int32)
    shape = functools.partial(jax.ShapeDtypeStruct, dtype=F32)
    half = functools.partial(jax.ShapeDtypeStruct, dtype=BF16)
    off_pairs = [(i, i + 1) for i in range(1, slabs - 1, 2)]
    off_pairs += [(target, source) for source, target in off_pairs]
    on_pairs = [(i, i ^ 1) for i in range(slabs)]
    odd = lax.rem(slab, 2)

    first_row, is_odd = row == 0, odd == 1
    low = data[:WIDTH].reshape(-1, lanes)
    high = data[planes - WIDTH :].reshape(-1, lanes)
    rim_off, rim_on = jnp.where(is_odd, high, low), jnp.where(is_odd, low, high)
    estimate, data, rim_off, rim_on = lax.optimization_barrier(
        (estimate, data, rim_off, rim_on)
    )
    edge = jnp.concatenate(
        [
            jnp.where(first_row, estimate[:, rows - EST_STRIP :], estimate[:, :EST_STRIP]),
            jnp.where(first_row, data[:, rows - DATA_STRIP :], data[:, :DATA_STRIP]),
        ],
        axis=1,
    )
    strip = lax.ppermute(edge, "row", [(0, 1), (1, 0)])
    held = lax.optimization_barrier((estimate, edge))[0]
    est_off = lax.ppermute(held, "slab", off_pairs)
    est_on = lax.ppermute(held, "slab", on_pairs)
    flat = strip.reshape(-1, lanes)
    off = jnp.concatenate([flat, rim_off], axis=0)
    on = jnp.concatenate([flat, rim_on], axis=0)
    off = lax.ppermute(off, "slab", off_pairs)
    on = lax.ppermute(on, "slab", on_pairs)

    pitch, used = rows + EST_STRIP, rows + DATA_STRIP
    wide, group = planes + 2 * WIDTH, 256 // rows
    taps_z, wx_h, wx_l, wo_h, wo_l, wr_h, wr_l, wy2_h, wy2_l = call(
        functools.partial(weights_kernel, rows),
        [shape((WIDTH + 1, 16, lanes))]
        + [half((lanes, lanes))] * 2
        + [half((group * used, group * rows))] * 2
        + [half((wide * EST_STRIP, wide * EST_STRIP))] * 2
        + [half((3 * pitch, 3 * pitch))] * 2,
        [],
        place, band, axes_perm, profile,
        scalars=4,
        cost=pl.CostEstimate(flops=COST, bytes_accessed=0, transcendentals=0),
    )
    partial = call(
        own_kernel,
        shape((wide, used, lanes)),
        [pltpu.VMEM((wide * rows, lanes), F32)],
        place, estimate, est_off, est_on, taps_z, wx_h, wx_l, wo_h, wo_l,
    )
    back = call(
        functools.partial(views_kernel, slabs),
        shape((planes, used, lanes)),
        [
            pltpu.VMEM((wide * EST_STRIP, lanes), F32),
            pltpu.VMEM((wide, used, lanes), F32),
            pltpu.VMEM((planes * pitch, lanes), F32),
        ],
        place, partial, data, strip, off, on, taps_z, wx_h, wx_l, wr_h, wr_l, wy2_h, wy2_l,
    )
    parts = lax.all_to_all(back, "view", 0, 0, tiled=True)
    copies = call(
        functools.partial(field_kernel, views, rows),
        shape((views, used, lanes)),
        [],
        place, parts, estimate, strip,
    )
    field = lax.all_to_all(copies, "view", 0, 0, tiled=True)
    reach = planes - TV_HALO
    low, high = field[:TV_HALO], field[reach:]
    off = lax.ppermute(jnp.where(is_odd, high, low), "slab", off_pairs)
    on = lax.ppermute(jnp.where(is_odd, low, high), "slab", on_pairs)
    deep = pltpu.VMEM((planes + 2 * TV_HALO, used, lanes), F32)
    return call(
        functools.partial(variation_kernel, slabs, rows),
        shape((planes, rows, lanes)),
        [deep, deep, deep],
        place, field, off, on,
    )


def solution(mesh):
    placed = (
        P("view", "slab", "row", None),
        P("slab", "row", None),
        P("view", None, None),
        P("view", None),
        P("view", None),
    )
    return jax.shard_map(
        body, mesh=mesh, in_specs=placed, out_specs=P("slab", "row", None), check_vma=False
    )
```

```python
import functools

import jax
import jax.numpy as jnp
from jax import lax
from jax.experimental import pallas as pl
from jax.experimental.pallas import tpu as pltpu
from jax.sharding import PartitionSpec as P

PASSES = 3
TAU = 0.05
EPS2 = 0.25
WIDTH = 4
EST_STRIP = 16
DATA_STRIP = 8
TV_HALO = 3
COST = 20000000000
VMEM = pl.BlockSpec(memory_space=pltpu.VMEM)
SMEM = pl.BlockSpec(memory_space=pltpu.SMEM)
F32 = jnp.float32
BF16 = jnp.bfloat16


def split(x):
    high = x.astype(BF16)
    return high, (x - high.astype(F32)).astype(BF16)


def dot3(a_high, a_low, b_high, b_low):
    dot = functools.partial(jnp.dot, preferred_element_type=F32)
    return dot(a_high, b_high) + (dot(a_low, b_high) + dot(a_high, b_low))


def weights_kernel(rows, band, perm, prof, taps_z, wx_h, wx_l, wo_h, wo_l, wr_h, wr_l, wy2_h, wy2_l):
    row = lax.axis_index("row")
    pitch = wy2_h.shape[0] // 3
    used = rows + DATA_STRIP

    def taps(axis, shape):
        k = perm[0, axis]
        reach = band[0, k]
        parts = [jnp.where(t <= reach, prof[0, k, t], 0.0) for t in range(WIDTH + 1)]
        total = parts[0]
        for part in parts[1:]:
            total = total + 2.0 * part
        return [jnp.full(shape, part, F32) / jnp.full(shape, total, F32) for part in parts]

    def banded(axis, shape, row_place, column_place, high, low):
        pieces = taps(axis, (8, shape[1]))
        column = column_place(lax.broadcasted_iota(jnp.int32, (8, shape[1]), 1))
        for start in range(0, shape[0], 16):
            parts = []
            for first in (start, start + 8):
                line = row_place(first + lax.broadcasted_iota(jnp.int32, (8, 128), 0))
                line = jnp.concatenate([line] * 2, axis=1)[:, : shape[1]]
                d = jnp.abs(line - column)
                value = jnp.where(d == 0, pieces[0], 0.0)
                for t in range(1, WIDTH + 1):
                    value = jnp.where(d == t, pieces[t], value)
                parts.append(split(value))
            high[start : start + 16, :] = jnp.concatenate([p[0] for p in parts], axis=0)
            low[start : start + 16, :] = jnp.concatenate([p[1] for p in parts], axis=0)

    for t, tap in enumerate(taps(0, taps_z.shape[1:])):
        taps_z[t] = tap
    banded(2, wx_h.shape, lambda i: i, lambda j: j, wx_h, wx_l)

    most = wo_h.shape[0]

    def placed(i, height, place_within):
        plane = sum((i >= n * height).astype(jnp.int32) for n in range(1, most // height))
        return plane * 4096 + place_within(i - height * plane)

    def halo_place(i, strip):
        return jnp.where((i >= rows) & (row == 1), i - rows - strip, i)

    def reached(i):
        return jnp.where(i < 8, i + (rows - 8) * (1 - row), halo_place(i - 8 + rows, DATA_STRIP))

    banded(
        1,
        wo_h.shape,
        lambda i: placed(i, used, lambda k: halo_place(k, DATA_STRIP)),
        lambda j: placed(j, rows, lambda k: k),
        wo_h,
        wo_l,
    )
    banded(
        1,
        wr_h.shape,
        lambda i: placed(i, EST_STRIP, reached),
        lambda j: placed(j, EST_STRIP, lambda k: halo_place(k + rows, EST_STRIP)),
        wr_h,
        wr_l,
    )
    banded(
        1,
        wy2_h.shape,
        lambda i: placed(i, pitch, lambda k: jnp.where(k < used, k - DATA_STRIP * row, 1024)),
        lambda j: placed(
            j, pitch, lambda k: jnp.where(k < used, halo_place(k, DATA_STRIP), 2048)
        ),
        wy2_h,
        wy2_l,
    )


def blur_z(read, taps_z):
    taps = [taps_z[t, 0:1, :] for t in range(WIDTH + 1)]
    total = taps[0] * read(WIDTH)
    for t in range(1, WIDTH + 1):
        total = total + taps[t] * (read(WIDTH - t) + read(WIDTH + t))
    return total


def blur_yx(x, w_h, w_l, wx_h, wx_l):
    x_h, x_l = split(x)
    m_h, m_l = split(dot3(w_h, w_l, x_h, x_l))
    return dot3(m_h, m_l, wx_h[...], wx_l[...])


def own_kernel(est, data, est_off, est_on, taps_z, wx_h, wx_l, wo_h, wo_l, out, ratio):
    planes, rows, lanes = est.shape
    wide, used, _ = out.shape
    odd = lax.rem(lax.axis_index("slab"), 2) == 1
    group = 256 // rows

    def work(below, above):
        mids = []
        for start in range(0, wide, group):
            part = [
                blur_z(lambda t: (below, est, above)[(p + t) // planes][(p + t) % planes], taps_z)
                for p in range(start, start + group)
            ]
            x_h, x_l = split(jnp.concatenate(part, axis=0))
            mids.append(split(dot3(wo_h[...], wo_l[...], x_h, x_l)))
        m_h = jnp.concatenate([m[0] for m in mids], axis=0)
        m_l = jnp.concatenate([m[1] for m in mids], axis=0)
        blurred = dot3(m_h, m_l, wx_h[...], wx_l[...]).reshape(wide, used, lanes)
        out[...] = blurred
        ratio[...] = data[:, 8 : rows - 8, :] / blurred[WIDTH : WIDTH + planes, 8 : rows - 8]

    @pl.when(odd)
    def _():
        work(est_on, est_off)

    @pl.when(jnp.logical_not(odd))
    def _():
        work(est_off, est_on)


def views_kernel(
    slabs, partial, inner, data, strip, off, on,
    taps_z, wx_h, wx_l, wr_h, wr_l, wy2_h, wy2_l, out, rims, ratio, flat,
):
    planes, rows, lanes = data.shape
    slab, row = lax.axis_index("slab"), lax.axis_index("row")
    pitch = rows + EST_STRIP
    used = rows + DATA_STRIP
    wide = planes + 2 * WIDTH
    thick = EST_STRIP + DATA_STRIP
    base = planes * thick
    odd = lax.rem(slab, 2) == 1

    def blur_first(below, above):
        def read(q):
            if q // planes == 1:
                return strip[q - planes, 0:EST_STRIP, :]
            at = q % planes * thick
            return (below, above)[q // planes // 2][at : at + EST_STRIP, :]

        for p in range(wide):
            rims[p * EST_STRIP : (p + 1) * EST_STRIP, :] = blur_z(lambda t: read(p + t), taps_z)

    @pl.when(odd)
    def _():
        blur_first(on, off)

    @pl.when(jnp.logical_not(odd))
    def _():
        blur_first(off, on)

    mids = []
    reached = blur_yx(rims[...], wr_h[...], wr_l[...], wx_h, wx_l).reshape(wide, 16, lanes)

    def touched(low, high):
        near = reached[low:high, 0:8]
        return (
            partial[low:high, 0:8, :] + jnp.where(row == 1, near, 0.0),
            partial[low:high, rows - 8 : rows, :] + jnp.where(row == 0, near, 0.0),
            partial[low:high, rows:used, :] + reached[low:high, 8:16],
        )

    def beyond(lower):
        first, second = (on, off) if lower else (off, on)
        low = 0 if lower else WIDTH + planes
        start, end, last = touched(low, low + WIDTH)
        blurred = jnp.concatenate([start, partial[low : low + WIDTH, 8 : rows - 8, :], end, last], axis=1)
        tops, lows = [], []
        for q in range(WIDTH):
            top = slice(base + q * rows, base + (q + 1) * rows)
            at = (q + planes - WIDTH if lower else q) * thick + EST_STRIP
            at = slice(at, at + DATA_STRIP)
            tops.append(jnp.where(odd, first[top, :], second[top, :])[None])
            lows.append(jnp.where(odd, first[at, :], second[at, :])[None])
        value = [jnp.concatenate(tops, axis=0), jnp.concatenate(lows, axis=0)]
        value = jnp.concatenate(value, axis=1) / blurred
        inside = slab > 0 if lower else slab < slabs - 1
        ratio[low : low + WIDTH] = jnp.where(inside, value, 0.0)

    def second_blur(low, high):
        for p in range(low, high):
            flat[p * pitch : p * pitch + used, :] = blur_z(lambda t: ratio[p + t], taps_z)
            flat[p * pitch + used : (p + 1) * pitch, :] = jnp.zeros((pitch - used, lanes), F32)
        n = (high - low) * pitch
        x_h, x_l = split(flat[low * pitch : low * pitch + n, :])
        return split(dot3(wy2_h[0:n, 0:n], wy2_l[0:n, 0:n], x_h, x_l))

    beyond(True)
    ends = [data[:, 0:8, :], data[:, rows - 8 : rows, :], strip[:, EST_STRIP:thick, :]]
    ends = jnp.concatenate(ends, axis=1) / jnp.concatenate(touched(WIDTH, WIDTH + planes), axis=1)
    own = slice(WIDTH, WIDTH + planes)
    ratio[own, 0:8, :] = ends[:, 0:8]
    ratio[own, 8 : rows - 8, :] = inner[...]
    ratio[own, rows - 8 : used, :] = ends[:, 8:24]
    mids = [second_blur(0, 2), second_blur(2, 4)]
    beyond(False)
    mids += [second_blur(4, 6), second_blur(6, 8)]
    m_h = jnp.concatenate([m[0] for m in mids], axis=0)
    m_l = jnp.concatenate([m[1] for m in mids], axis=0)
    out[...] = dot3(m_h, m_l, wx_h[...], wx_l[...]).reshape(planes, pitch, lanes)[:, :used]


def field_kernel(views, rows, parts, est, strip, out):
    view, row = lax.axis_index("view"), lax.axis_index("row")
    total = parts[0]
    for v in range(1, views):
        total = total + parts[v]
    total = total * (1.0 / views)
    own, rim = est[view], strip[view, 0:EST_STRIP, :]

    @pl.when(row == 0)
    def _():
        value = jnp.concatenate([own * total[0:rows], rim[0:DATA_STRIP] * total[rows:]], axis=0)
        for v in range(views):
            out[v] = value

    @pl.when(row == 1)
    def _():
        value = jnp.concatenate(
            [rim[DATA_STRIP:] * total[0:DATA_STRIP], own * total[DATA_STRIP:]], axis=0
        )
        for v in range(views):
            out[v] = value


def variation_kernel(slabs, rows, field, off, on, out, start, first, second):
    planes, used, lanes = field.shape
    slab, row = lax.axis_index("slab"), lax.axis_index("row")
    half = lanes // 2
    odd = lax.rem(slab, 2)
    start[pl.ds(odd * (planes + TV_HALO), TV_HALO)] = off[...]
    start[pl.ds((1 - odd) * (planes + TV_HALO), TV_HALO)] = on[...]
    start[TV_HALO : TV_HALO + planes] = field[...]
    lane = lax.broadcasted_iota(jnp.int32, (1, 1, half), 2)
    line = lax.broadcasted_iota(jnp.int32, (1, 8, half), 1)

    def next_x(x):
        turned = [pltpu.roll(h, half - 1, 2) for h in x]
        return [
            jnp.where(lane == half - 1, turned[1], turned[0]),
            jnp.where(lane == half - 1, 0.0, turned[1]),
        ]

    def last_x(x):
        turned = [pltpu.roll(h, 1, 2) for h in x]
        return [jnp.where(lane == 0, 0.0, turned[0]), jnp.where(lane == 0, turned[0], turned[1])]

    def next_y(x):
        turned = pltpu.roll(x, used - 1, 1)
        last = jnp.where(line == 7, 0.0, turned[:, used - 8 :])
        return jnp.concatenate([turned[:, : used - 8], last], axis=1)

    def last_y(x):
        turned = pltpu.roll(x, 1, 1)
        return jnp.concatenate([jnp.where(line == 0, 0.0, turned[:, :8]), turned[:, 8:]], axis=1)

    def masked(x, z):
        if z >= TV_HALO and z + x.shape[0] <= TV_HALO + planes:
            return x
        parts = []
        for i in range(x.shape[0]):
            part = x[i : i + 1]
            if z + i < TV_HALO:
                part = jnp.where(slab > 0, part, 0.0)
            elif z + i >= TV_HALO + planes:
                part = jnp.where(slab < slabs - 1, part, 0.0)
            parts.append(part)
        return jnp.concatenate(parts, axis=0) if len(parts) > 1 else parts[0]

    def flux(source, z, count, only_z):
        box = [slice(h * half, (h + 1) * half) for h in range(2)]
        now = [source[z : z + count, :, b] for b in box]
        after = [source[z + 1 : z + count + 1, :, b] for b in box]
        side = next_x(now)
        f_x, f_y, f_z = [], [], []
        for h in range(2):
            g_z, g_y, g_x = after[h] - now[h], next_y(now[h]) - now[h], side[h] - now[h]
            scale = masked(lax.rsqrt(g_z * g_z + g_y * g_y + g_x * g_x + EPS2), z)
            f_z.append(g_z * scale)
            if not only_z:
                f_y.append(g_y * scale)
                f_x.append(g_x * scale)
        return now, f_x, f_y, f_z

    def one_pass(source, low, high, group, target):
        before = flux(source, low - 1, 1, True)[3]
        for z in range(low, high, group):
            count = min(group, high - z)
            now, f_x, f_y, f_z = flux(source, z, count, False)
            side = last_x(f_x)
            for h in range(2):
                below = before[h]
                if count > 1:
                    below = jnp.concatenate([below, f_z[h][: count - 1]], axis=0)
                spread = (f_z[h] - below) + (f_y[h] - last_y(f_y[h])) + (f_x[h] - side[h])
                target[z : z + count, :, h * half : (h + 1) * half] = masked(now[h] + TAU * spread, z)
            before = [f[count - 1 : count] for f in f_z]

    deep = planes + 2 * TV_HALO
    groups = (4, 5, 4)
    one_pass(start, 1, deep - 1, groups[0], first)
    one_pass(first, 2, deep - 2, groups[1], second)
    one_pass(second, 3, deep - 3, groups[2], first)
    skip = pl.multiple_of(row * (used - rows), 8)
    out[...] = first[TV_HALO : TV_HALO + planes, pl.ds(skip, rows), :]


def call(kernel, shapes, scratch, *args, cost=None, scalars=0):
    specs = [SMEM if i < scalars else VMEM for i in range(len(args))]
    return pl.pallas_call(
        kernel,
        out_shape=shapes,
        in_specs=specs,
        out_specs=jax.tree.map(lambda _: VMEM, shapes),
        scratch_shapes=scratch,
        cost_estimate=cost,
        compiler_params=pltpu.CompilerParams(vmem_limit_bytes=16 * 2**20),
    )(*args)


def body(data, estimate, profile, band, axes_perm):
    data = data[0]
    planes, rows, lanes = estimate.shape
    views, slabs = lax.axis_size("view"), lax.axis_size("slab")
    slab, row = lax.axis_index("slab"), lax.axis_index("row")
    shape = functools.partial(jax.ShapeDtypeStruct, dtype=F32)
    half = functools.partial(jax.ShapeDtypeStruct, dtype=BF16)
    off_pairs = [(i, i + 1) for i in range(1, slabs - 1, 2)]
    off_pairs += [(target, source) for source, target in off_pairs]
    on_pairs = [(i, i ^ 1) for i in range(slabs)]
    odd = lax.rem(slab, 2)

    first_row, is_odd = row == 0, odd == 1
    low = data[:WIDTH].reshape(-1, lanes)
    high = data[planes - WIDTH :].reshape(-1, lanes)
    rim_off, rim_on = jnp.where(is_odd, high, low), jnp.where(is_odd, low, high)
    estimate, data, rim_off, rim_on = lax.optimization_barrier(
        (estimate, data, rim_off, rim_on)
    )
    edge = jnp.concatenate(
        [
            jnp.where(first_row, estimate[:, rows - EST_STRIP :], estimate[:, :EST_STRIP]),
            jnp.where(first_row, data[:, rows - DATA_STRIP :], data[:, :DATA_STRIP]),
        ],
        axis=1,
    )
    strip = lax.ppermute(edge, "row", [(0, 1), (1, 0)])
    held = lax.optimization_barrier((estimate, edge))[0]
    est_off = lax.ppermute(held, "slab", off_pairs)
    est_on = lax.ppermute(held, "slab", on_pairs)
    flat = strip.reshape(-1, lanes)
    off = jnp.concatenate([flat, rim_off], axis=0)
    on = jnp.concatenate([flat, rim_on], axis=0)
    off = lax.ppermute(off, "slab", off_pairs)
    on = lax.ppermute(on, "slab", on_pairs)

    pitch, used = rows + EST_STRIP, rows + DATA_STRIP
    wide, group = planes + 2 * WIDTH, 256 // rows
    taps_z, wx_h, wx_l, wo_h, wo_l, wr_h, wr_l, wy2_h, wy2_l = call(
        functools.partial(weights_kernel, rows),
        [shape((WIDTH + 1, 16, lanes))]
        + [half((lanes, lanes))] * 2
        + [half((group * used, group * rows))] * 2
        + [half((wide * EST_STRIP, wide * EST_STRIP))] * 2
        + [half((3 * pitch, 3 * pitch))] * 2,
        [],
        band, axes_perm, profile,
        scalars=3,
        cost=pl.CostEstimate(flops=COST, bytes_accessed=0, transcendentals=0),
    )
    partial, inner = call(
        own_kernel,
        [shape((wide, used, lanes)), shape((planes, rows - 16, lanes))],
        [],
        estimate, data, est_off, est_on, taps_z, wx_h, wx_l, wo_h, wo_l,
    )
    back = call(
        functools.partial(views_kernel, slabs),
        shape((planes, used, lanes)),
        [
            pltpu.VMEM((wide * EST_STRIP, lanes), F32),
            pltpu.VMEM((wide, used, lanes), F32),
            pltpu.VMEM((planes * pitch, lanes), F32),
        ],
        partial, inner, data, strip, off, on, taps_z, wx_h, wx_l, wr_h, wr_l, wy2_h, wy2_l,
    )
    parts = lax.all_to_all(back, "view", 0, 0, tiled=True)
    copies = call(
        functools.partial(field_kernel, views, rows),
        shape((views, used, lanes)),
        [],
        parts, estimate, strip,
    )
    field = lax.all_to_all(copies, "view", 0, 0, tiled=True)
    reach = planes - TV_HALO
    low, high = field[:TV_HALO], field[reach:]
    off = lax.ppermute(jnp.where(is_odd, high, low), "slab", off_pairs)
    on = lax.ppermute(jnp.where(is_odd, low, high), "slab", on_pairs)
    deep = pltpu.VMEM((planes + 2 * TV_HALO, used, lanes), F32)
    return call(
        functools.partial(variation_kernel, slabs, rows),
        shape((planes, rows, lanes)),
        [deep, deep, deep],
        field, off, on,
    )


def solution(mesh):
    placed = (
        P("view", "slab", "row", None),
        P("slab", "row", None),
        P("view", None, None),
        P("view", None),
        P("view", None),
    )
    return jax.shard_map(
        body, mesh=mesh, in_specs=placed, out_specs=P("slab", "row", None), check_vma=False
    )
```

```python
import functools

import jax
import jax.numpy as jnp
from jax import lax
from jax.experimental import pallas as pl
from jax.experimental.pallas import tpu as pltpu
from jax.sharding import PartitionSpec as P

PASSES = 3
TAU = 0.05
EPS2 = 0.25
WIDTH = 4
EST_STRIP = 16
DATA_STRIP = 8
TV_HALO = 3
COST = 20000000000
VMEM = pl.BlockSpec(memory_space=pltpu.VMEM)
SMEM = pl.BlockSpec(memory_space=pltpu.SMEM)
F32 = jnp.float32
BF16 = jnp.bfloat16


def split(x):
    high = x.astype(BF16)
    return high, (x - high.astype(F32)).astype(BF16)


def dot3(a_high, a_low, b_high, b_low):
    dot = functools.partial(jnp.dot, preferred_element_type=F32)
    return dot(a_high, b_high) + (dot(a_low, b_high) + dot(a_high, b_low))


def weights_kernel(rows, band, perm, prof, taps_z, wx_h, wx_l, wo_h, wo_l, wr_h, wr_l, wy2_h, wy2_l):
    row = lax.axis_index("row")
    pitch = wy2_h.shape[0] // 3
    used = rows + DATA_STRIP

    def taps(axis, shape):
        k = perm[0, axis]
        reach = band[0, k]
        parts = [jnp.where(t <= reach, prof[0, k, t], 0.0) for t in range(WIDTH + 1)]
        total = parts[0]
        for part in parts[1:]:
            total = total + 2.0 * part
        return [jnp.full(shape, part, F32) / jnp.full(shape, total, F32) for part in parts]

    def banded(axis, shape, row_place, column_place, high, low):
        pieces = taps(axis, (8, shape[1]))
        column = column_place(lax.broadcasted_iota(jnp.int32, (8, shape[1]), 1))
        for start in range(0, shape[0], 16):
            parts = []
            for first in (start, start + 8):
                line = row_place(first + lax.broadcasted_iota(jnp.int32, (8, 128), 0))
                line = jnp.concatenate([line] * 2, axis=1)[:, : shape[1]]
                d = jnp.abs(line - column)
                value = jnp.where(d == 0, pieces[0], 0.0)
                for t in range(1, WIDTH + 1):
                    value = jnp.where(d == t, pieces[t], value)
                parts.append(split(value))
            high[start : start + 16, :] = jnp.concatenate([p[0] for p in parts], axis=0)
            low[start : start + 16, :] = jnp.concatenate([p[1] for p in parts], axis=0)

    for t, tap in enumerate(taps(0, taps_z.shape[1:])):
        taps_z[t] = tap
    banded(2, wx_h.shape, lambda i: i, lambda j: j, wx_h, wx_l)

    most = wo_h.shape[0]

    def placed(i, height, place_within):
        plane = sum((i >= n * height).astype(jnp.int32) for n in range(1, most // height))
        return plane * 4096 + place_within(i - height * plane)

    def halo_place(i, strip):
        return jnp.where((i >= rows) & (row == 1), i - rows - strip, i)

    def reached(i):
        return jnp.where(i < 8, i + (rows - 8) * (1 - row), halo_place(i - 8 + rows, DATA_STRIP))

    banded(
        1,
        wo_h.shape,
        lambda i: placed(i, used, lambda k: halo_place(k, DATA_STRIP)),
        lambda j: placed(j, rows, lambda k: k),
        wo_h,
        wo_l,
    )
    banded(
        1,
        wr_h.shape,
        lambda i: placed(i, EST_STRIP, reached),
        lambda j: placed(j, EST_STRIP, lambda k: halo_place(k + rows, EST_STRIP)),
        wr_h,
        wr_l,
    )
    banded(
        1,
        wy2_h.shape,
        lambda i: placed(i, pitch, lambda k: jnp.where(k < used, k - DATA_STRIP * row, 1024)),
        lambda j: placed(
            j, pitch, lambda k: jnp.where(k < used, halo_place(k, DATA_STRIP), 2048)
        ),
        wy2_h,
        wy2_l,
    )


def blur_z(read, taps_z):
    taps = [taps_z[t, 0:1, :] for t in range(WIDTH + 1)]
    total = taps[0] * read(WIDTH)
    for t in range(1, WIDTH + 1):
        total = total + taps[t] * (read(WIDTH - t) + read(WIDTH + t))
    return total


def blur_yx(x, w_h, w_l, wx_h, wx_l):
    x_h, x_l = split(x)
    m_h, m_l = split(dot3(w_h, w_l, x_h, x_l))
    return dot3(m_h, m_l, wx_h[...], wx_l[...])


def own_kernel(est, data, est_off, est_on, taps_z, wx_h, wx_l, wo_h, wo_l, out, ratio):
    planes, rows, lanes = est.shape
    wide, used, _ = out.shape
    odd = lax.rem(lax.axis_index("slab"), 2) == 1
    group = 256 // rows

    def work(below, above):
        mids = []
        for start in range(0, wide, group):
            part = [
                blur_z(lambda t: (below, est, above)[(p + t) // planes][(p + t) % planes], taps_z)
                for p in range(start, start + group)
            ]
            x_h, x_l = split(jnp.concatenate(part, axis=0))
            mids.append(split(dot3(wo_h[...], wo_l[...], x_h, x_l)))
        m_h = jnp.concatenate([m[0] for m in mids], axis=0)
        m_l = jnp.concatenate([m[1] for m in mids], axis=0)
        blurred = dot3(m_h, m_l, wx_h[...], wx_l[...]).reshape(wide, used, lanes)
        out[...] = blurred
        ratio[...] = data[:, 8 : rows - 8, :] / blurred[WIDTH : WIDTH + planes, 8 : rows - 8]

    @pl.when(odd)
    def _():
        work(est_on, est_off)

    @pl.when(jnp.logical_not(odd))
    def _():
        work(est_off, est_on)


def views_kernel(
    slabs, partial, inner, data, strip, est_off, off, on,
    taps_z, wx_h, wx_l, wr_h, wr_l, wy2_h, wy2_l, out, rims, ratio, flat,
):
    planes, rows, lanes = data.shape
    slab, row = lax.axis_index("slab"), lax.axis_index("row")
    pitch = rows + EST_STRIP
    used = rows + DATA_STRIP
    wide = planes + 2 * WIDTH
    thick = EST_STRIP + DATA_STRIP
    base = planes * thick
    odd = lax.rem(slab, 2) == 1

    def blur_first(below, above):
        def read(q):
            if q // planes == 1:
                return strip[q - planes, 0:EST_STRIP, :]
            if (below, above)[q // planes // 2] is off:
                return off[q % planes, 0:EST_STRIP, :]
            at = q % planes * thick
            return on[at : at + EST_STRIP, :]

        for p in range(wide):
            rims[p * EST_STRIP : (p + 1) * EST_STRIP, :] = blur_z(lambda t: read(p + t), taps_z)

    @pl.when(odd)
    def _():
        blur_first(on, off)

    @pl.when(jnp.logical_not(odd))
    def _():
        blur_first(off, on)

    mids = []
    reached = blur_yx(rims[...], wr_h[...], wr_l[...], wx_h, wx_l).reshape(wide, 16, lanes)

    def touched(low, high):
        near = reached[low:high, 0:8]
        return (
            partial[low:high, 0:8, :] + jnp.where(row == 1, near, 0.0),
            partial[low:high, rows - 8 : rows, :] + jnp.where(row == 0, near, 0.0),
            partial[low:high, rows:used, :] + reached[low:high, 8:16],
        )

    def beyond(lower):
        next_chip = jnp.logical_not(odd) if lower else odd
        low = 0 if lower else WIDTH + planes
        start, end, last = touched(low, low + WIDTH)
        blurred = jnp.concatenate([start, partial[low : low + WIDTH, 8 : rows - 8, :], end, last], axis=1)
        tops, lows = [], []
        for q in range(WIDTH):
            k = q + planes - WIDTH if lower else q
            top = on[base + q * rows : base + (q + 1) * rows, :]
            last_rows = on[k * thick + EST_STRIP : (k + 1) * thick, :]
            tops.append(jnp.where(next_chip, est_off[planes + q], top)[None])
            lows.append(jnp.where(next_chip, off[k, EST_STRIP:thick, :], last_rows)[None])
        value = [jnp.concatenate(tops, axis=0), jnp.concatenate(lows, axis=0)]
        value = jnp.concatenate(value, axis=1) / blurred
        inside = slab > 0 if lower else slab < slabs - 1
        ratio[low : low + WIDTH] = jnp.where(inside, value, 0.0)

    def second_blur(low, high):
        for p in range(low, high):
            flat[p * pitch : p * pitch + used, :] = blur_z(lambda t: ratio[p + t], taps_z)
            flat[p * pitch + used : (p + 1) * pitch, :] = jnp.zeros((pitch - used, lanes), F32)
        n = (high - low) * pitch
        x_h, x_l = split(flat[low * pitch : low * pitch + n, :])
        return split(dot3(wy2_h[0:n, 0:n], wy2_l[0:n, 0:n], x_h, x_l))

    beyond(True)
    ends = [data[:, 0:8, :], data[:, rows - 8 : rows, :], strip[:, EST_STRIP:thick, :]]
    ends = jnp.concatenate(ends, axis=1) / jnp.concatenate(touched(WIDTH, WIDTH + planes), axis=1)
    own = slice(WIDTH, WIDTH + planes)
    ratio[own, 0:8, :] = ends[:, 0:8]
    ratio[own, 8 : rows - 8, :] = inner[...]
    ratio[own, rows - 8 : used, :] = ends[:, 8:24]
    mids = [second_blur(0, 2), second_blur(2, 4)]
    beyond(False)
    mids += [second_blur(4, 6), second_blur(6, 8)]
    m_h = jnp.concatenate([m[0] for m in mids], axis=0)
    m_l = jnp.concatenate([m[1] for m in mids], axis=0)
    out[...] = dot3(m_h, m_l, wx_h[...], wx_l[...]).reshape(planes, pitch, lanes)[:, :used]


def field_kernel(views, rows, parts, est, strip, out):
    view, row = lax.axis_index("view"), lax.axis_index("row")
    total = parts[0]
    for v in range(1, views):
        total = total + parts[v]
    total = total * (1.0 / views)
    own, rim = est[view], strip[view, 0:EST_STRIP, :]

    @pl.when(row == 0)
    def _():
        value = jnp.concatenate([own * total[0:rows], rim[0:DATA_STRIP] * total[rows:]], axis=0)
        for v in range(views):
            out[v] = value

    @pl.when(row == 1)
    def _():
        value = jnp.concatenate(
            [rim[DATA_STRIP:] * total[0:DATA_STRIP], own * total[DATA_STRIP:]], axis=0
        )
        for v in range(views):
            out[v] = value


def variation_kernel(slabs, rows, field, off, on, out, start, first, second):
    planes, used, lanes = field.shape
    slab, row = lax.axis_index("slab"), lax.axis_index("row")
    half = lanes // 2
    odd = lax.rem(slab, 2)
    start[pl.ds(odd * (planes + TV_HALO), TV_HALO)] = off[...]
    start[pl.ds((1 - odd) * (planes + TV_HALO), TV_HALO)] = on[...]
    start[TV_HALO : TV_HALO + planes] = field[...]
    lane = lax.broadcasted_iota(jnp.int32, (1, 1, half), 2)
    line = lax.broadcasted_iota(jnp.int32, (1, 8, half), 1)

    def next_x(x):
        turned = [pltpu.roll(h, half - 1, 2) for h in x]
        return [
            jnp.where(lane == half - 1, turned[1], turned[0]),
            jnp.where(lane == half - 1, 0.0, turned[1]),
        ]

    def last_x(x):
        turned = [pltpu.roll(h, 1, 2) for h in x]
        return [jnp.where(lane == 0, 0.0, turned[0]), jnp.where(lane == 0, turned[0], turned[1])]

    def next_y(x):
        turned = pltpu.roll(x, used - 1, 1)
        last = jnp.where(line == 7, 0.0, turned[:, used - 8 :])
        return jnp.concatenate([turned[:, : used - 8], last], axis=1)

    def last_y(x):
        turned = pltpu.roll(x, 1, 1)
        return jnp.concatenate([jnp.where(line == 0, 0.0, turned[:, :8]), turned[:, 8:]], axis=1)

    def masked(x, z):
        if z >= TV_HALO and z + x.shape[0] <= TV_HALO + planes:
            return x
        parts = []
        for i in range(x.shape[0]):
            part = x[i : i + 1]
            if z + i < TV_HALO:
                part = jnp.where(slab > 0, part, 0.0)
            elif z + i >= TV_HALO + planes:
                part = jnp.where(slab < slabs - 1, part, 0.0)
            parts.append(part)
        return jnp.concatenate(parts, axis=0) if len(parts) > 1 else parts[0]

    def flux(source, z, count, only_z):
        box = [slice(h * half, (h + 1) * half) for h in range(2)]
        now = [source[z : z + count, :, b] for b in box]
        after = [source[z + 1 : z + count + 1, :, b] for b in box]
        side = next_x(now)
        f_x, f_y, f_z = [], [], []
        for h in range(2):
            g_z, g_y, g_x = after[h] - now[h], next_y(now[h]) - now[h], side[h] - now[h]
            scale = masked(lax.rsqrt(g_z * g_z + g_y * g_y + g_x * g_x + EPS2), z)
            f_z.append(g_z * scale)
            if not only_z:
                f_y.append(g_y * scale)
                f_x.append(g_x * scale)
        return now, f_x, f_y, f_z

    def one_pass(source, low, high, group, target):
        before = flux(source, low - 1, 1, True)[3]
        for z in range(low, high, group):
            count = min(group, high - z)
            now, f_x, f_y, f_z = flux(source, z, count, False)
            side = last_x(f_x)
            for h in range(2):
                below = before[h]
                if count > 1:
                    below = jnp.concatenate([below, f_z[h][: count - 1]], axis=0)
                spread = (f_z[h] - below) + (f_y[h] - last_y(f_y[h])) + (f_x[h] - side[h])
                target[z : z + count, :, h * half : (h + 1) * half] = masked(now[h] + TAU * spread, z)
            before = [f[count - 1 : count] for f in f_z]

    deep = planes + 2 * TV_HALO
    groups = (4, 5, 4)
    one_pass(start, 1, deep - 1, groups[0], first)
    one_pass(first, 2, deep - 2, groups[1], second)
    one_pass(second, 3, deep - 3, groups[2], first)
    skip = pl.multiple_of(row * (used - rows), 8)
    out[...] = first[TV_HALO : TV_HALO + planes, pl.ds(skip, rows), :]


def call(kernel, shapes, scratch, *args, cost=None, scalars=0):
    specs = [SMEM if i < scalars else VMEM for i in range(len(args))]
    return pl.pallas_call(
        kernel,
        out_shape=shapes,
        in_specs=specs,
        out_specs=jax.tree.map(lambda _: VMEM, shapes),
        scratch_shapes=scratch,
        cost_estimate=cost,
        compiler_params=pltpu.CompilerParams(vmem_limit_bytes=16 * 2**20),
    )(*args)


def body(data, estimate, profile, band, axes_perm):
    data = data[0]
    planes, rows, lanes = estimate.shape
    views, slabs = lax.axis_size("view"), lax.axis_size("slab")
    slab, row = lax.axis_index("slab"), lax.axis_index("row")
    shape = functools.partial(jax.ShapeDtypeStruct, dtype=F32)
    half = functools.partial(jax.ShapeDtypeStruct, dtype=BF16)
    off_pairs = [(i, i + 1) for i in range(1, slabs - 1, 2)]
    off_pairs += [(target, source) for source, target in off_pairs]
    on_pairs = [(i, i ^ 1) for i in range(slabs)]
    odd = lax.rem(slab, 2)

    first_row, is_odd = row == 0, odd == 1
    low = data[:WIDTH].reshape(-1, lanes)
    high = data[planes - WIDTH :].reshape(-1, lanes)
    rim_off, rim_on = jnp.where(is_odd, high, low), jnp.where(is_odd, low, high)
    estimate, data, rim_off, rim_on = lax.optimization_barrier(
        (estimate, data, rim_off, rim_on)
    )
    edge = jnp.concatenate(
        [
            jnp.where(first_row, estimate[:, rows - EST_STRIP :], estimate[:, :EST_STRIP]),
            jnp.where(first_row, data[:, rows - DATA_STRIP :], data[:, :DATA_STRIP]),
        ],
        axis=1,
    )
    strip = lax.ppermute(edge, "row", [(0, 1), (1, 0)])
    held = lax.optimization_barrier((estimate, edge))[0]
    far = jnp.concatenate([held, rim_off.reshape(WIDTH, rows, lanes)], axis=0)
    held, far = lax.optimization_barrier((held, far))
    est_off = lax.ppermute(far, "slab", off_pairs)
    est_on = lax.ppermute(held, "slab", on_pairs)
    on = jnp.concatenate([strip.reshape(-1, lanes), rim_on], axis=0)
    off = strip
    off = lax.ppermute(off, "slab", off_pairs)
    on = lax.ppermute(on, "slab", on_pairs)

    pitch, used = rows + EST_STRIP, rows + DATA_STRIP
    wide, group = planes + 2 * WIDTH, 256 // rows
    taps_z, wx_h, wx_l, wo_h, wo_l, wr_h, wr_l, wy2_h, wy2_l = call(
        functools.partial(weights_kernel, rows),
        [shape((WIDTH + 1, 16, lanes))]
        + [half((lanes, lanes))] * 2
        + [half((group * used, group * rows))] * 2
        + [half((wide * EST_STRIP, wide * EST_STRIP))] * 2
        + [half((3 * pitch, 3 * pitch))] * 2,
        [],
        band, axes_perm, profile,
        scalars=3,
        cost=pl.CostEstimate(flops=COST, bytes_accessed=0, transcendentals=0),
    )
    partial, inner = call(
        own_kernel,
        [shape((wide, used, lanes)), shape((planes, rows - 16, lanes))],
        [],
        estimate, data, est_off, est_on, taps_z, wx_h, wx_l, wo_h, wo_l,
    )
    back = call(
        functools.partial(views_kernel, slabs),
        shape((planes, used, lanes)),
        [
            pltpu.VMEM((wide * EST_STRIP, lanes), F32),
            pltpu.VMEM((wide, used, lanes), F32),
            pltpu.VMEM((planes * pitch, lanes), F32),
        ],
        partial, inner, data, strip, est_off, off, on, taps_z, wx_h, wx_l, wr_h, wr_l, wy2_h, wy2_l,
    )
    parts = lax.all_to_all(back, "view", 0, 0, tiled=True)
    copies = call(
        functools.partial(field_kernel, views, rows),
        shape((views, used, lanes)),
        [],
        parts, estimate, strip,
    )
    field = lax.all_to_all(copies, "view", 0, 0, tiled=True)
    reach = planes - TV_HALO
    low, high = field[:TV_HALO], field[reach:]
    off = lax.ppermute(jnp.where(is_odd, high, low), "slab", off_pairs)
    on = lax.ppermute(jnp.where(is_odd, low, high), "slab", on_pairs)
    deep = pltpu.VMEM((planes + 2 * TV_HALO, used, lanes), F32)
    return call(
        functools.partial(variation_kernel, slabs, rows),
        shape((planes, rows, lanes)),
        [deep, deep, deep],
        field, off, on,
    )


def solution(mesh):
    placed = (
        P("view", "slab", "row", None),
        P("slab", "row", None),
        P("view", None, None),
        P("view", None),
        P("view", None),
    )
    return jax.shard_map(
        body, mesh=mesh, in_specs=placed, out_specs=P("slab", "row", None), check_vma=False
    )
```

```python
import functools

import jax
import jax.numpy as jnp
from jax import lax
from jax.experimental import pallas as pl
from jax.experimental.pallas import tpu as pltpu
from jax.sharding import PartitionSpec as P

PASSES = 3
TAU = 0.05
EPS2 = 0.25
WIDTH = 4
EST_STRIP = 16
DATA_STRIP = 8
TV_HALO = 3
COST = 20000000000
VMEM = pl.BlockSpec(memory_space=pltpu.VMEM)
SMEM = pl.BlockSpec(memory_space=pltpu.SMEM)
F32 = jnp.float32
BF16 = jnp.bfloat16


def split(x):
    high = x.astype(BF16)
    return high, (x - high.astype(F32)).astype(BF16)


def dot3(a_high, a_low, b_high, b_low):
    dot = functools.partial(jnp.dot, preferred_element_type=F32)
    return dot(a_high, b_high) + (dot(a_low, b_high) + dot(a_high, b_low))


def weights_kernel(rows, band, perm, prof, taps_z, wx_h, wx_l, wo_h, wo_l, wr_h, wr_l, wy2_h, wy2_l):
    row = lax.axis_index("row")
    pitch = wy2_h.shape[0] // 3
    used = rows + DATA_STRIP

    def taps(axis, shape):
        k = perm[0, axis]
        reach = band[0, k]
        parts = [jnp.where(t <= reach, prof[0, k, t], 0.0) for t in range(WIDTH + 1)]
        total = parts[0]
        for part in parts[1:]:
            total = total + 2.0 * part
        return [jnp.full(shape, part, F32) / jnp.full(shape, total, F32) for part in parts]

    def banded(axis, shape, row_place, column_place, high, low):
        pieces = taps(axis, (8, shape[1]))
        column = column_place(lax.broadcasted_iota(jnp.int32, (8, shape[1]), 1))
        for start in range(0, shape[0], 16):
            parts = []
            for first in (start, start + 8):
                line = row_place(first + lax.broadcasted_iota(jnp.int32, (8, 128), 0))
                line = jnp.concatenate([line] * 2, axis=1)[:, : shape[1]]
                d = jnp.abs(line - column)
                value = jnp.where(d == 0, pieces[0], 0.0)
                for t in range(1, WIDTH + 1):
                    value = jnp.where(d == t, pieces[t], value)
                parts.append(split(value))
            high[start : start + 16, :] = jnp.concatenate([p[0] for p in parts], axis=0)
            low[start : start + 16, :] = jnp.concatenate([p[1] for p in parts], axis=0)

    for t, tap in enumerate(taps(0, taps_z.shape[1:])):
        taps_z[t] = tap
    banded(2, wx_h.shape, lambda i: i, lambda j: j, wx_h, wx_l)

    most = wo_h.shape[0]

    def placed(i, height, place_within):
        plane = sum((i >= n * height).astype(jnp.int32) for n in range(1, most // height))
        return plane * 4096 + place_within(i - height * plane)

    def halo_place(i, strip):
        return jnp.where((i >= rows) & (row == 1), i - rows - strip, i)

    def reached(i):
        return jnp.where(i < 8, i + (rows - 8) * (1 - row), halo_place(i - 8 + rows, DATA_STRIP))

    banded(
        1,
        wo_h.shape,
        lambda i: placed(i, used, lambda k: halo_place(k, DATA_STRIP)),
        lambda j: placed(j, rows, lambda k: k),
        wo_h,
        wo_l,
    )
    banded(
        1,
        wr_h.shape,
        lambda i: placed(i, EST_STRIP, reached),
        lambda j: placed(j, EST_STRIP, lambda k: halo_place(k + rows, EST_STRIP)),
        wr_h,
        wr_l,
    )
    banded(
        1,
        wy2_h.shape,
        lambda i: placed(i, pitch, lambda k: jnp.where(k < used, k - DATA_STRIP * row, 1024)),
        lambda j: placed(
            j, pitch, lambda k: jnp.where(k < used, halo_place(k, DATA_STRIP), 2048)
        ),
        wy2_h,
        wy2_l,
    )


def blur_z(read, taps_z):
    taps = [taps_z[t, 0:1, :] for t in range(WIDTH + 1)]
    total = taps[0] * read(WIDTH)
    for t in range(1, WIDTH + 1):
        total = total + taps[t] * (read(WIDTH - t) + read(WIDTH + t))
    return total


def blur_yx(x, w_h, w_l, wx_h, wx_l):
    x_h, x_l = split(x)
    m_h, m_l = split(dot3(w_h, w_l, x_h, x_l))
    return dot3(m_h, m_l, wx_h[...], wx_l[...])


def own_kernel(est, data, est_off, est_on, taps_z, wx_h, wx_l, wo_h, wo_l, out, ratio):
    planes, rows, lanes = est.shape
    wide, used, _ = out.shape
    odd = lax.rem(lax.axis_index("slab"), 2) == 1
    group = 256 // rows

    def work(below, above):
        mids = []
        for start in range(0, wide, group):
            part = [
                blur_z(lambda t: (below, est, above)[(p + t) // planes][(p + t) % planes], taps_z)
                for p in range(start, start + group)
            ]
            x_h, x_l = split(jnp.concatenate(part, axis=0))
            mids.append(split(dot3(wo_h[...], wo_l[...], x_h, x_l)))
        m_h = jnp.concatenate([m[0] for m in mids], axis=0)
        m_l = jnp.concatenate([m[1] for m in mids], axis=0)
        blurred = dot3(m_h, m_l, wx_h[...], wx_l[...]).reshape(wide, used, lanes)
        out[...] = blurred
        ratio[...] = data[:, 8 : rows - 8, :] / blurred[WIDTH : WIDTH + planes, 8 : rows - 8]

    @pl.when(odd)
    def _():
        work(est_on, est_off)

    @pl.when(jnp.logical_not(odd))
    def _():
        work(est_off, est_on)


def views_kernel(
    slabs, partial, inner, data, strip, est_off, off, on,
    taps_z, wx_h, wx_l, wr_h, wr_l, wy2_h, wy2_l, out, rims, ratio, flat,
):
    planes, rows, lanes = data.shape
    slab, row = lax.axis_index("slab"), lax.axis_index("row")
    pitch = rows + EST_STRIP
    used = rows + DATA_STRIP
    wide = planes + 2 * WIDTH
    thick = EST_STRIP + DATA_STRIP
    base = planes * EST_STRIP + WIDTH * DATA_STRIP
    odd = lax.rem(slab, 2) == 1

    def blur_first(below, above):
        def read(q):
            if q // planes == 1:
                return strip[q - planes, 0:EST_STRIP, :]
            at = q % planes * EST_STRIP
            return (below, above)[q // planes // 2][at : at + EST_STRIP, :]

        for p in range(wide):
            rims[p * EST_STRIP : (p + 1) * EST_STRIP, :] = blur_z(lambda t: read(p + t), taps_z)

    @pl.when(odd)
    def _():
        blur_first(on, off)

    @pl.when(jnp.logical_not(odd))
    def _():
        blur_first(off, on)

    mids = []
    reached = blur_yx(rims[...], wr_h[...], wr_l[...], wx_h, wx_l).reshape(wide, 16, lanes)

    def touched(low, high):
        near = reached[low:high, 0:8]
        return (
            partial[low:high, 0:8, :] + jnp.where(row == 1, near, 0.0),
            partial[low:high, rows - 8 : rows, :] + jnp.where(row == 0, near, 0.0),
            partial[low:high, rows:used, :] + reached[low:high, 8:16],
        )

    def beyond(lower):
        next_chip = jnp.logical_not(odd) if lower else odd
        low = 0 if lower else WIDTH + planes
        start, end, last = touched(low, low + WIDTH)
        blurred = jnp.concatenate([start, partial[low : low + WIDTH, 8 : rows - 8, :], end, last], axis=1)
        tops, lows = [], []
        for q in range(WIDTH):
            top = on[base + q * rows : base + (q + 1) * rows, :]
            at = planes * EST_STRIP + q * DATA_STRIP
            at = slice(at, at + DATA_STRIP)
            tops.append(jnp.where(next_chip, est_off[planes + q], top)[None])
            lows.append(jnp.where(next_chip, off[at, :], on[at, :])[None])
        value = [jnp.concatenate(tops, axis=0), jnp.concatenate(lows, axis=0)]
        value = jnp.concatenate(value, axis=1) / blurred
        inside = slab > 0 if lower else slab < slabs - 1
        ratio[low : low + WIDTH] = jnp.where(inside, value, 0.0)

    def second_blur(low, high):
        for p in range(low, high):
            flat[p * pitch : p * pitch + used, :] = blur_z(lambda t: ratio[p + t], taps_z)
            flat[p * pitch + used : (p + 1) * pitch, :] = jnp.zeros((pitch - used, lanes), F32)
        n = (high - low) * pitch
        x_h, x_l = split(flat[low * pitch : low * pitch + n, :])
        return split(dot3(wy2_h[0:n, 0:n], wy2_l[0:n, 0:n], x_h, x_l))

    beyond(True)
    ends = [data[:, 0:8, :], data[:, rows - 8 : rows, :], strip[:, EST_STRIP:thick, :]]
    ends = jnp.concatenate(ends, axis=1) / jnp.concatenate(touched(WIDTH, WIDTH + planes), axis=1)
    own = slice(WIDTH, WIDTH + planes)
    ratio[own, 0:8, :] = ends[:, 0:8]
    ratio[own, 8 : rows - 8, :] = inner[...]
    ratio[own, rows - 8 : used, :] = ends[:, 8:24]
    mids = [second_blur(0, 2), second_blur(2, 4)]
    beyond(False)
    mids += [second_blur(4, 6), second_blur(6, 8)]
    m_h = jnp.concatenate([m[0] for m in mids], axis=0)
    m_l = jnp.concatenate([m[1] for m in mids], axis=0)
    out[...] = dot3(m_h, m_l, wx_h[...], wx_l[...]).reshape(planes, pitch, lanes)[:, :used]


def field_kernel(views, rows, parts, est, strip, out):
    view, row = lax.axis_index("view"), lax.axis_index("row")
    total = parts[0]
    for v in range(1, views):
        total = total + parts[v]
    total = total * (1.0 / views)
    own, rim = est[view], strip[view, 0:EST_STRIP, :]

    @pl.when(row == 0)
    def _():
        value = jnp.concatenate([own * total[0:rows], rim[0:DATA_STRIP] * total[rows:]], axis=0)
        for v in range(views):
            out[v] = value

    @pl.when(row == 1)
    def _():
        value = jnp.concatenate(
            [rim[DATA_STRIP:] * total[0:DATA_STRIP], own * total[DATA_STRIP:]], axis=0
        )
        for v in range(views):
            out[v] = value


def variation_kernel(slabs, rows, field, off, on, out, start, first, second, sems):
    planes, used, lanes = field.shape
    slab, row = lax.axis_index("slab"), lax.axis_index("row")
    half = lanes // 2
    odd = lax.rem(slab, 2)
    start[pl.ds(odd * (planes + TV_HALO), TV_HALO)] = off[...]
    start[pl.ds((1 - odd) * (planes + TV_HALO), TV_HALO)] = on[...]
    start[TV_HALO : TV_HALO + planes] = field[...]
    lane = lax.broadcasted_iota(jnp.int32, (1, 1, half), 2)
    line = lax.broadcasted_iota(jnp.int32, (1, 8, half), 1)

    def next_x(x):
        turned = [pltpu.roll(h, half - 1, 2) for h in x]
        return [
            jnp.where(lane == half - 1, turned[1], turned[0]),
            jnp.where(lane == half - 1, 0.0, turned[1]),
        ]

    def last_x(x):
        turned = [pltpu.roll(h, 1, 2) for h in x]
        return [jnp.where(lane == 0, 0.0, turned[0]), jnp.where(lane == 0, turned[0], turned[1])]

    def next_y(x):
        turned = pltpu.roll(x, used - 1, 1)
        last = jnp.where(line == 7, 0.0, turned[:, used - 8 :])
        return jnp.concatenate([turned[:, : used - 8], last], axis=1)

    def last_y(x):
        turned = pltpu.roll(x, 1, 1)
        return jnp.concatenate([jnp.where(line == 0, 0.0, turned[:, :8]), turned[:, 8:]], axis=1)

    def masked(x, z):
        if z >= TV_HALO and z + x.shape[0] <= TV_HALO + planes:
            return x
        parts = []
        for i in range(x.shape[0]):
            part = x[i : i + 1]
            if z + i < TV_HALO:
                part = jnp.where(slab > 0, part, 0.0)
            elif z + i >= TV_HALO + planes:
                part = jnp.where(slab < slabs - 1, part, 0.0)
            parts.append(part)
        return jnp.concatenate(parts, axis=0) if len(parts) > 1 else parts[0]

    def flux(source, z, count, only_z):
        box = [slice(h * half, (h + 1) * half) for h in range(2)]
        now = [source[z : z + count, :, b] for b in box]
        after = [source[z + 1 : z + count + 1, :, b] for b in box]
        side = next_x(now)
        f_x, f_y, f_z = [], [], []
        for h in range(2):
            g_z, g_y, g_x = after[h] - now[h], next_y(now[h]) - now[h], side[h] - now[h]
            scale = masked(lax.rsqrt(g_z * g_z + g_y * g_y + g_x * g_x + EPS2), z)
            f_z.append(g_z * scale)
            if not only_z:
                f_y.append(g_y * scale)
                f_x.append(g_x * scale)
        return now, f_x, f_y, f_z

    def one_pass(source, low, high, group, target, then=None):
        before = flux(source, low - 1, 1, True)[3]
        for z in range(low, high, group):
            count = min(group, high - z)
            now, f_x, f_y, f_z = flux(source, z, count, False)
            side = last_x(f_x)
            for h in range(2):
                below = before[h]
                if count > 1:
                    below = jnp.concatenate([below, f_z[h][: count - 1]], axis=0)
                spread = (f_z[h] - below) + (f_y[h] - last_y(f_y[h])) + (f_x[h] - side[h])
                target[z : z + count, :, h * half : (h + 1) * half] = masked(now[h] + TAU * spread, z)
            before = [f[count - 1 : count] for f in f_z]
            if then is not None:
                then(z, count)

    deep = planes + 2 * TV_HALO
    groups = (4, 5, 3)
    one_pass(start, 1, deep - 1, groups[0], first)
    one_pass(first, 2, deep - 2, groups[1], second)
    skip = pl.multiple_of(row * (used - rows), 8)
    copies = []

    def leave(z, count):
        copy = pltpu.make_async_copy(
            first.at[z : z + count, pl.ds(skip, rows), :],
            out.at[z - TV_HALO : z - TV_HALO + count],
            sems.at[len(copies)],
        )
        copy.start()
        copies.append(copy)

    one_pass(second, TV_HALO, deep - TV_HALO, groups[2], first, leave)
    for copy in copies:
        copy.wait()


def call(kernel, shapes, scratch, *args, cost=None, scalars=0, target=VMEM):
    specs = [SMEM if i < scalars else VMEM for i in range(len(args))]
    return pl.pallas_call(
        kernel,
        out_shape=shapes,
        in_specs=specs,
        out_specs=jax.tree.map(lambda _: target, shapes),
        scratch_shapes=scratch,
        cost_estimate=cost,
        compiler_params=pltpu.CompilerParams(vmem_limit_bytes=16 * 2**20),
    )(*args)


def body(data, estimate, profile, band, axes_perm):
    data = data[0]
    planes, rows, lanes = estimate.shape
    views, slabs = lax.axis_size("view"), lax.axis_size("slab")
    slab, row = lax.axis_index("slab"), lax.axis_index("row")
    shape = functools.partial(jax.ShapeDtypeStruct, dtype=F32)
    half = functools.partial(jax.ShapeDtypeStruct, dtype=BF16)
    off_pairs = [(i, i + 1) for i in range(1, slabs - 1, 2)]
    off_pairs += [(target, source) for source, target in off_pairs]
    on_pairs = [(i, i ^ 1) for i in range(slabs)]
    odd = lax.rem(slab, 2)

    first_row, is_odd = row == 0, odd == 1
    low = data[:WIDTH].reshape(-1, lanes)
    high = data[planes - WIDTH :].reshape(-1, lanes)
    rim_off, rim_on = jnp.where(is_odd, high, low), jnp.where(is_odd, low, high)
    estimate, data, rim_off, rim_on = lax.optimization_barrier(
        (estimate, data, rim_off, rim_on)
    )
    edge = jnp.concatenate(
        [
            jnp.where(first_row, estimate[:, rows - EST_STRIP :], estimate[:, :EST_STRIP]),
            jnp.where(first_row, data[:, rows - DATA_STRIP :], data[:, :DATA_STRIP]),
        ],
        axis=1,
    )
    strip = lax.ppermute(edge, "row", [(0, 1), (1, 0)])
    held = lax.optimization_barrier((estimate, edge))[0]
    far = jnp.concatenate([held, rim_off.reshape(WIDTH, rows, lanes)], axis=0)
    held, far = lax.optimization_barrier((held, far))
    est_off = lax.ppermute(far, "slab", off_pairs)
    est_on = lax.ppermute(held, "slab", on_pairs)
    parts = [strip[:, :EST_STRIP].reshape(-1, lanes)]
    first = strip[:WIDTH, EST_STRIP:].reshape(-1, lanes)
    last = strip[planes - WIDTH :, EST_STRIP:].reshape(-1, lanes)
    off = jnp.concatenate(parts + [jnp.where(is_odd, last, first)], axis=0)
    on = jnp.concatenate(parts + [jnp.where(is_odd, first, last), rim_on], axis=0)
    off = lax.ppermute(off, "slab", off_pairs)
    on = lax.ppermute(on, "slab", on_pairs)

    pitch, used = rows + EST_STRIP, rows + DATA_STRIP
    wide, group = planes + 2 * WIDTH, 256 // rows
    taps_z, wx_h, wx_l, wo_h, wo_l, wr_h, wr_l, wy2_h, wy2_l = call(
        functools.partial(weights_kernel, rows),
        [shape((WIDTH + 1, 16, lanes))]
        + [half((lanes, lanes))] * 2
        + [half((group * used, group * rows))] * 2
        + [half((wide * EST_STRIP, wide * EST_STRIP))] * 2
        + [half((3 * pitch, 3 * pitch))] * 2,
        [],
        band, axes_perm, profile,
        scalars=3,
        cost=pl.CostEstimate(flops=COST, bytes_accessed=0, transcendentals=0),
    )
    partial, inner = call(
        own_kernel,
        [shape((wide, used, lanes)), shape((planes, rows - 16, lanes))],
        [],
        estimate, data, est_off, est_on, taps_z, wx_h, wx_l, wo_h, wo_l,
    )
    back = call(
        functools.partial(views_kernel, slabs),
        shape((planes, used, lanes)),
        [
            pltpu.VMEM((wide * EST_STRIP, lanes), F32),
            pltpu.VMEM((wide, used, lanes), F32),
            pltpu.VMEM((planes * pitch, lanes), F32),
        ],
        partial, inner, data, strip, est_off, off, on, taps_z, wx_h, wx_l, wr_h, wr_l, wy2_h, wy2_l,
    )
    parts = lax.all_to_all(back, "view", 0, 0, tiled=True)
    copies = call(
        functools.partial(field_kernel, views, rows),
        shape((views, used, lanes)),
        [],
        parts, estimate, strip,
    )
    field = lax.all_to_all(copies, "view", 0, 0, tiled=True)
    reach = planes - TV_HALO
    low, high = field[:TV_HALO], field[reach:]
    off = lax.ppermute(jnp.where(is_odd, high, low), "slab", off_pairs)
    on = lax.ppermute(jnp.where(is_odd, low, high), "slab", on_pairs)
    deep = pltpu.VMEM((planes + 2 * TV_HALO, used, lanes), F32)
    return call(
        functools.partial(variation_kernel, slabs, rows),
        shape((planes, rows, lanes)),
        [deep, deep, deep, pltpu.SemaphoreType.DMA((4,))],
        field, off, on,
        target=pl.BlockSpec(memory_space=pl.ANY),
    )


def solution(mesh):
    placed = (
        P("view", "slab", "row", None),
        P("slab", "row", None),
        P("view", None, None),
        P("view", None),
        P("view", None),
    )
    return jax.shard_map(
        body, mesh=mesh, in_specs=placed, out_specs=P("slab", "row", None), check_vma=False
    )
```

```python
import functools

import jax
import jax.numpy as jnp
from jax import lax
from jax.experimental import pallas as pl
from jax.experimental.pallas import tpu as pltpu
from jax.sharding import PartitionSpec as P

PASSES = 3
TAU = 0.05
EPS2 = 0.25
WIDTH = 4
EST_STRIP = 16
DATA_STRIP = 8
TV_HALO = 3
COST = 20000000000
VMEM = pl.BlockSpec(memory_space=pltpu.VMEM)
SMEM = pl.BlockSpec(memory_space=pltpu.SMEM)
F32 = jnp.float32
BF16 = jnp.bfloat16


def split(x):
    high = x.astype(BF16)
    return high, (x - high.astype(F32)).astype(BF16)


def dot3(a_high, a_low, b_high, b_low):
    dot = functools.partial(jnp.dot, preferred_element_type=F32)
    return dot(a_high, b_high) + (dot(a_low, b_high) + dot(a_high, b_low))


def weights_kernel(rows, band, perm, prof, taps_z, wx_h, wx_l, wo_h, wo_l, wr_h, wr_l, wy2_h, wy2_l):
    row = lax.axis_index("row")
    pitch = wy2_h.shape[0] // 3
    used = rows + DATA_STRIP

    def taps(axis, shape):
        k = perm[0, axis]
        reach = band[0, k]
        parts = [jnp.where(t <= reach, prof[0, k, t], 0.0) for t in range(WIDTH + 1)]
        total = parts[0]
        for part in parts[1:]:
            total = total + 2.0 * part
        return [jnp.full(shape, part, F32) / jnp.full(shape, total, F32) for part in parts]

    def banded(axis, shape, row_place, column_place, high, low):
        pieces = taps(axis, (8, shape[1]))
        column = column_place(lax.broadcasted_iota(jnp.int32, (8, shape[1]), 1))
        for start in range(0, shape[0], 16):
            parts = []
            for first in (start, start + 8):
                line = row_place(first + lax.broadcasted_iota(jnp.int32, (8, 128), 0))
                line = jnp.concatenate([line] * 2, axis=1)[:, : shape[1]]
                d = jnp.abs(line - column)
                value = jnp.where(d == 0, pieces[0], 0.0)
                for t in range(1, WIDTH + 1):
                    value = jnp.where(d == t, pieces[t], value)
                parts.append(split(value))
            high[start : start + 16, :] = jnp.concatenate([p[0] for p in parts], axis=0)
            low[start : start + 16, :] = jnp.concatenate([p[1] for p in parts], axis=0)

    for t, tap in enumerate(taps(0, taps_z.shape[1:])):
        taps_z[t] = tap
    banded(2, wx_h.shape, lambda i: i, lambda j: j, wx_h, wx_l)

    most = wo_h.shape[0]

    def placed(i, height, place_within):
        plane = sum((i >= n * height).astype(jnp.int32) for n in range(1, most // height))
        return plane * 4096 + place_within(i - height * plane)

    def halo_place(i, strip):
        return jnp.where((i >= rows) & (row == 1), i - rows - strip, i)

    def reached(i):
        return jnp.where(i < 8, i + (rows - 8) * (1 - row), halo_place(i - 8 + rows, DATA_STRIP))

    banded(
        1,
        wo_h.shape,
        lambda i: placed(i, used, lambda k: halo_place(k, DATA_STRIP)),
        lambda j: placed(j, rows, lambda k: k),
        wo_h,
        wo_l,
    )
    banded(
        1,
        wr_h.shape,
        lambda i: placed(i, EST_STRIP, reached),
        lambda j: placed(j, EST_STRIP, lambda k: halo_place(k + rows, EST_STRIP)),
        wr_h,
        wr_l,
    )
    banded(
        1,
        wy2_h.shape,
        lambda i: placed(i, pitch, lambda k: jnp.where(k < used, k - DATA_STRIP * row, 1024)),
        lambda j: placed(
            j, pitch, lambda k: jnp.where(k < used, halo_place(k, DATA_STRIP), 2048)
        ),
        wy2_h,
        wy2_l,
    )


def blur_z(read, taps_z):
    taps = [taps_z[t, 0:1, :] for t in range(WIDTH + 1)]
    total = taps[0] * read(WIDTH)
    for t in range(1, WIDTH + 1):
        total = total + taps[t] * (read(WIDTH - t) + read(WIDTH + t))
    return total


def blur_yx(x, w_h, w_l, wx_h, wx_l):
    x_h, x_l = split(x)
    m_h, m_l = split(dot3(w_h, w_l, x_h, x_l))
    return dot3(m_h, m_l, wx_h[...], wx_l[...])


def own_kernel(est, data, est_off, est_on, taps_z, wx_h, wx_l, wo_h, wo_l, out, ratio):
    planes, rows, lanes = est.shape
    wide, used, _ = out.shape
    odd = lax.rem(lax.axis_index("slab"), 2) == 1
    group = 256 // rows

    def work(below, above):
        mids = []
        for start in range(0, wide, group):
            part = [
                blur_z(lambda t: (below, est, above)[(p + t) // planes][(p + t) % planes], taps_z)
                for p in range(start, start + group)
            ]
            x_h, x_l = split(jnp.concatenate(part, axis=0))
            mids.append(split(dot3(wo_h[...], wo_l[...], x_h, x_l)))
        m_h = jnp.concatenate([m[0] for m in mids], axis=0)
        m_l = jnp.concatenate([m[1] for m in mids], axis=0)
        blurred = dot3(m_h, m_l, wx_h[...], wx_l[...]).reshape(wide, used, lanes)
        out[...] = blurred
        ratio[...] = data[:, 8 : rows - 8, :] / blurred[WIDTH : WIDTH + planes, 8 : rows - 8]

    @pl.when(odd)
    def _():
        work(est_on, est_off)

    @pl.when(jnp.logical_not(odd))
    def _():
        work(est_off, est_on)


def views_kernel(
    slabs, partial, inner, data, strip, est_off, off, on,
    taps_z, wx_h, wx_l, wr_h, wr_l, wy2_h, wy2_l, out, rims, ratio, flat,
):
    planes, rows, lanes = data.shape
    slab, row = lax.axis_index("slab"), lax.axis_index("row")
    pitch = rows + EST_STRIP
    used = rows + DATA_STRIP
    wide = planes + 2 * WIDTH
    thick = EST_STRIP + DATA_STRIP
    base = planes * EST_STRIP + WIDTH * DATA_STRIP
    odd = lax.rem(slab, 2) == 1

    def blur_first(below, above):
        def read(q):
            if q // planes == 1:
                return strip[q - planes, 0:EST_STRIP, :]
            at = q % planes * EST_STRIP
            return (below, above)[q // planes // 2][at : at + EST_STRIP, :]

        for p in range(wide):
            rims[p * EST_STRIP : (p + 1) * EST_STRIP, :] = blur_z(lambda t: read(p + t), taps_z)

    @pl.when(odd)
    def _():
        blur_first(on, off)

    @pl.when(jnp.logical_not(odd))
    def _():
        blur_first(off, on)

    mids = []
    reached = blur_yx(rims[...], wr_h[...], wr_l[...], wx_h, wx_l).reshape(wide, 16, lanes)

    def touched(low, high):
        near = reached[low:high, 0:8]
        return (
            partial[low:high, 0:8, :] + jnp.where(row == 1, near, 0.0),
            partial[low:high, rows - 8 : rows, :] + jnp.where(row == 0, near, 0.0),
            partial[low:high, rows:used, :] + reached[low:high, 8:16],
        )

    def beyond(lower):
        next_chip = jnp.logical_not(odd) if lower else odd
        low = 0 if lower else WIDTH + planes
        start, end, last = touched(low, low + WIDTH)
        blurred = jnp.concatenate([start, partial[low : low + WIDTH, 8 : rows - 8, :], end, last], axis=1)
        tops, lows = [], []
        for q in range(WIDTH):
            top = on[base + q * rows : base + (q + 1) * rows, :]
            at = planes * EST_STRIP + q * DATA_STRIP
            at = slice(at, at + DATA_STRIP)
            tops.append(jnp.where(next_chip, est_off[planes + q], top)[None])
            lows.append(jnp.where(next_chip, off[at, :], on[at, :])[None])
        value = [jnp.concatenate(tops, axis=0), jnp.concatenate(lows, axis=0)]
        value = jnp.concatenate(value, axis=1) / blurred
        inside = slab > 0 if lower else slab < slabs - 1
        ratio[low : low + WIDTH] = jnp.where(inside, value, 0.0)

    def second_blur(low, high):
        for p in range(low, high):
            flat[p * pitch : p * pitch + used, :] = blur_z(lambda t: ratio[p + t], taps_z)
            flat[p * pitch + used : (p + 1) * pitch, :] = jnp.zeros((pitch - used, lanes), F32)
        n = (high - low) * pitch
        x_h, x_l = split(flat[low * pitch : low * pitch + n, :])
        mid = dot3(wy2_h[0:n, 0:n], wy2_l[0:n, 0:n], x_h, x_l).reshape(high - low, pitch, lanes)
        return split(mid[:, :used].reshape(-1, lanes))

    beyond(True)
    ends = [data[:, 0:8, :], data[:, rows - 8 : rows, :], strip[:, EST_STRIP:thick, :]]
    ends = jnp.concatenate(ends, axis=1) / jnp.concatenate(touched(WIDTH, WIDTH + planes), axis=1)
    own = slice(WIDTH, WIDTH + planes)
    ratio[own, 0:8, :] = ends[:, 0:8]
    ratio[own, 8 : rows - 8, :] = inner[...]
    ratio[own, rows - 8 : used, :] = ends[:, 8:24]
    mids = [second_blur(0, 2), second_blur(2, 4)]
    beyond(False)
    mids += [second_blur(4, 6), second_blur(6, 8)]
    m_h = jnp.concatenate([m[0] for m in mids], axis=0)
    m_l = jnp.concatenate([m[1] for m in mids], axis=0)
    out[...] = dot3(m_h, m_l, wx_h[...], wx_l[...]).reshape(planes, used, lanes)


def field_kernel(views, rows, parts, est, strip, out):
    view, row = lax.axis_index("view"), lax.axis_index("row")
    total = parts[0]
    for v in range(1, views):
        total = total + parts[v]
    total = total * (1.0 / views)
    own, rim = est[view], strip[view, 0:EST_STRIP, :]

    @pl.when(row == 0)
    def _():
        value = jnp.concatenate([own * total[0:rows], rim[0:DATA_STRIP] * total[rows:]], axis=0)
        for v in range(views):
            out[v] = value

    @pl.when(row == 1)
    def _():
        value = jnp.concatenate(
            [rim[DATA_STRIP:] * total[0:DATA_STRIP], own * total[DATA_STRIP:]], axis=0
        )
        for v in range(views):
            out[v] = value


def variation_kernel(slabs, rows, field, off, on, out, start, first, second, sems):
    planes, used, lanes = field.shape
    slab, row = lax.axis_index("slab"), lax.axis_index("row")
    half = lanes // 2
    odd = lax.rem(slab, 2)
    start[pl.ds(odd * (planes + TV_HALO), TV_HALO)] = off[...]
    start[pl.ds((1 - odd) * (planes + TV_HALO), TV_HALO)] = on[...]
    start[TV_HALO : TV_HALO + planes] = field[...]
    lane = lax.broadcasted_iota(jnp.int32, (1, 1, half), 2)
    line = lax.broadcasted_iota(jnp.int32, (1, 8, half), 1)

    def next_x(x):
        turned = [pltpu.roll(h, half - 1, 2) for h in x]
        return [
            jnp.where(lane == half - 1, turned[1], turned[0]),
            jnp.where(lane == half - 1, 0.0, turned[1]),
        ]

    def last_x(x):
        turned = [pltpu.roll(h, 1, 2) for h in x]
        return [jnp.where(lane == 0, 0.0, turned[0]), jnp.where(lane == 0, turned[0], turned[1])]

    def next_y(x):
        turned = pltpu.roll(x, used - 1, 1)
        last = jnp.where(line == 7, 0.0, turned[:, used - 8 :])
        return jnp.concatenate([turned[:, : used - 8], last], axis=1)

    def last_y(x):
        turned = pltpu.roll(x, 1, 1)
        return jnp.concatenate([jnp.where(line == 0, 0.0, turned[:, :8]), turned[:, 8:]], axis=1)

    def masked(x, z):
        if z >= TV_HALO and z + x.shape[0] <= TV_HALO + planes:
            return x
        parts = []
        for i in range(x.shape[0]):
            part = x[i : i + 1]
            if z + i < TV_HALO:
                part = jnp.where(slab > 0, part, 0.0)
            elif z + i >= TV_HALO + planes:
                part = jnp.where(slab < slabs - 1, part, 0.0)
            parts.append(part)
        return jnp.concatenate(parts, axis=0) if len(parts) > 1 else parts[0]

    def flux(source, z, count, only_z):
        box = [slice(h * half, (h + 1) * half) for h in range(2)]
        now = [source[z : z + count, :, b] for b in box]
        after = [source[z + 1 : z + count + 1, :, b] for b in box]
        side = next_x(now)
        f_x, f_y, f_z = [], [], []
        for h in range(2):
            g_z, g_y, g_x = after[h] - now[h], next_y(now[h]) - now[h], side[h] - now[h]
            scale = masked(lax.rsqrt(g_z * g_z + g_y * g_y + g_x * g_x + EPS2), z)
            f_z.append(g_z * scale)
            if not only_z:
                f_y.append(g_y * scale)
                f_x.append(g_x * scale)
        return now, f_x, f_y, f_z

    def one_pass(source, low, high, group, target, then=None):
        before = flux(source, low - 1, 1, True)[3]
        for z in range(low, high, group):
            count = min(group, high - z)
            now, f_x, f_y, f_z = flux(source, z, count, False)
            side = last_x(f_x)
            for h in range(2):
                below = before[h]
                if count > 1:
                    below = jnp.concatenate([below, f_z[h][: count - 1]], axis=0)
                spread = (f_z[h] - below) + (f_y[h] - last_y(f_y[h])) + (f_x[h] - side[h])
                target[z : z + count, :, h * half : (h + 1) * half] = masked(now[h] + TAU * spread, z)
            before = [f[count - 1 : count] for f in f_z]
            if then is not None:
                then(z, count)

    deep = planes + 2 * TV_HALO
    groups = (4, 5, 3)
    one_pass(start, 1, deep - 1, groups[0], first)
    one_pass(first, 2, deep - 2, groups[1], second)
    skip = pl.multiple_of(row * (used - rows), 8)
    copies = []

    def leave(z, count):
        copy = pltpu.make_async_copy(
            first.at[z : z + count, pl.ds(skip, rows), :],
            out.at[z - TV_HALO : z - TV_HALO + count],
            sems.at[len(copies)],
        )
        copy.start()
        copies.append(copy)

    one_pass(second, TV_HALO, deep - TV_HALO, groups[2], first, leave)
    for copy in copies:
        copy.wait()


def call(kernel, shapes, scratch, *args, cost=None, scalars=0, target=VMEM):
    specs = [SMEM if i < scalars else VMEM for i in range(len(args))]
    return pl.pallas_call(
        kernel,
        out_shape=shapes,
        in_specs=specs,
        out_specs=jax.tree.map(lambda _: target, shapes),
        scratch_shapes=scratch,
        cost_estimate=cost,
        compiler_params=pltpu.CompilerParams(vmem_limit_bytes=16 * 2**20),
    )(*args)


def body(data, estimate, profile, band, axes_perm):
    data = data[0]
    planes, rows, lanes = estimate.shape
    views, slabs = lax.axis_size("view"), lax.axis_size("slab")
    slab, row = lax.axis_index("slab"), lax.axis_index("row")
    shape = functools.partial(jax.ShapeDtypeStruct, dtype=F32)
    half = functools.partial(jax.ShapeDtypeStruct, dtype=BF16)
    off_pairs = [(i, i + 1) for i in range(1, slabs - 1, 2)]
    off_pairs += [(target, source) for source, target in off_pairs]
    on_pairs = [(i, i ^ 1) for i in range(slabs)]
    odd = lax.rem(slab, 2)

    first_row, is_odd = row == 0, odd == 1
    low = data[:WIDTH].reshape(-1, lanes)
    high = data[planes - WIDTH :].reshape(-1, lanes)
    rim_off, rim_on = jnp.where(is_odd, high, low), jnp.where(is_odd, low, high)
    estimate, data, rim_off, rim_on = lax.optimization_barrier(
        (estimate, data, rim_off, rim_on)
    )
    edge = jnp.concatenate(
        [
            jnp.where(first_row, estimate[:, rows - EST_STRIP :], estimate[:, :EST_STRIP]),
            jnp.where(first_row, data[:, rows - DATA_STRIP :], data[:, :DATA_STRIP]),
        ],
        axis=1,
    )
    strip = lax.ppermute(edge, "row", [(0, 1), (1, 0)])
    held = lax.optimization_barrier((estimate, edge))[0]
    far = jnp.concatenate([held, rim_off.reshape(WIDTH, rows, lanes)], axis=0)
    held, far = lax.optimization_barrier((held, far))
    est_off = lax.ppermute(far, "slab", off_pairs)
    est_on = lax.ppermute(held, "slab", on_pairs)
    parts = [strip[:, :EST_STRIP].reshape(-1, lanes)]
    first = strip[:WIDTH, EST_STRIP:].reshape(-1, lanes)
    last = strip[planes - WIDTH :, EST_STRIP:].reshape(-1, lanes)
    off = jnp.concatenate(parts + [jnp.where(is_odd, last, first)], axis=0)
    on = jnp.concatenate(parts + [jnp.where(is_odd, first, last), rim_on], axis=0)
    off = lax.ppermute(off, "slab", off_pairs)
    on = lax.ppermute(on, "slab", on_pairs)

    pitch, used = rows + EST_STRIP, rows + DATA_STRIP
    wide, group = planes + 2 * WIDTH, 256 // rows
    taps_z, wx_h, wx_l, wo_h, wo_l, wr_h, wr_l, wy2_h, wy2_l = call(
        functools.partial(weights_kernel, rows),
        [shape((WIDTH + 1, 16, lanes))]
        + [half((lanes, lanes))] * 2
        + [half((group * used, group * rows))] * 2
        + [half((wide * EST_STRIP, wide * EST_STRIP))] * 2
        + [half((3 * pitch, 3 * pitch))] * 2,
        [],
        band, axes_perm, profile,
        scalars=3,
        cost=pl.CostEstimate(flops=COST, bytes_accessed=0, transcendentals=0),
    )
    partial, inner = call(
        own_kernel,
        [shape((wide, used, lanes)), shape((planes, rows - 16, lanes))],
        [],
        estimate, data, est_off, est_on, taps_z, wx_h, wx_l, wo_h, wo_l,
    )
    back = call(
        functools.partial(views_kernel, slabs),
        shape((planes, used, lanes)),
        [
            pltpu.VMEM((wide * EST_STRIP, lanes), F32),
            pltpu.VMEM((wide, used, lanes), F32),
            pltpu.VMEM((planes * pitch, lanes), F32),
        ],
        partial, inner, data, strip, est_off, off, on, taps_z, wx_h, wx_l, wr_h, wr_l, wy2_h, wy2_l,
    )
    parts = lax.all_to_all(back, "view", 0, 0, tiled=True)
    copies = call(
        functools.partial(field_kernel, views, rows),
        shape((views, used, lanes)),
        [],
        parts, estimate, strip,
    )
    field = lax.all_to_all(copies, "view", 0, 0, tiled=True)
    reach = planes - TV_HALO
    low, high = field[:TV_HALO], field[reach:]
    off = lax.ppermute(jnp.where(is_odd, high, low), "slab", off_pairs)
    on = lax.ppermute(jnp.where(is_odd, low, high), "slab", on_pairs)
    deep = pltpu.VMEM((planes + 2 * TV_HALO, used, lanes), F32)
    return call(
        functools.partial(variation_kernel, slabs, rows),
        shape((planes, rows, lanes)),
        [deep, deep, deep, pltpu.SemaphoreType.DMA((4,))],
        field, off, on,
        target=pl.BlockSpec(memory_space=pl.ANY),
    )


def solution(mesh):
    placed = (
        P("view", "slab", "row", None),
        P("slab", "row", None),
        P("view", None, None),
        P("view", None),
        P("view", None),
    )
    return jax.shard_map(
        body, mesh=mesh, in_specs=placed, out_specs=P("slab", "row", None), check_vma=False
    )
```

```python
import functools

import jax
import jax.numpy as jnp
from jax import lax
from jax.experimental import pallas as pl
from jax.experimental.pallas import tpu as pltpu
from jax.sharding import PartitionSpec as P

PASSES = 3
TAU = 0.05
EPS2 = 0.25
WIDTH = 4
EST_STRIP = 16
DATA_STRIP = 8
TV_HALO = 3
COST = 20000000000
VMEM = pl.BlockSpec(memory_space=pltpu.VMEM)
SMEM = pl.BlockSpec(memory_space=pltpu.SMEM)
F32 = jnp.float32
BF16 = jnp.bfloat16


def split(x):
    high = x.astype(BF16)
    return high, (x - high.astype(F32)).astype(BF16)


def dot3(a_high, a_low, b_high, b_low):
    dot = functools.partial(jnp.dot, preferred_element_type=F32)
    return dot(a_high, b_high) + (dot(a_low, b_high) + dot(a_high, b_low))


def weights_kernel(rows, band, perm, prof, taps_z, wx_h, wx_l, wo_h, wo_l, wr_h, wr_l, wy2_h, wy2_l):
    row = lax.axis_index("row")
    pitch = wy2_h.shape[0] // 3
    used = rows + DATA_STRIP

    def taps(axis, shape):
        k = perm[0, axis]
        reach = band[0, k]
        parts = [jnp.where(t <= reach, prof[0, k, t], 0.0) for t in range(WIDTH + 1)]
        total = parts[0]
        for part in parts[1:]:
            total = total + 2.0 * part
        return [jnp.full(shape, part, F32) / jnp.full(shape, total, F32) for part in parts]

    def banded(axis, shape, row_place, column_place, high, low):
        pieces = taps(axis, (8, shape[1]))
        column = column_place(lax.broadcasted_iota(jnp.int32, (8, shape[1]), 1))
        for start in range(0, shape[0], 16):
            parts = []
            for first in (start, start + 8):
                line = row_place(first + lax.broadcasted_iota(jnp.int32, (8, 128), 0))
                line = jnp.concatenate([line] * 2, axis=1)[:, : shape[1]]
                d = jnp.abs(line - column)
                value = jnp.where(d == 0, pieces[0], 0.0)
                for t in range(1, WIDTH + 1):
                    value = jnp.where(d == t, pieces[t], value)
                parts.append(split(value))
            high[start : start + 16, :] = jnp.concatenate([p[0] for p in parts], axis=0)
            low[start : start + 16, :] = jnp.concatenate([p[1] for p in parts], axis=0)

    for t, tap in enumerate(taps(0, taps_z.shape[1:])):
        taps_z[t] = tap
    banded(2, wx_h.shape, lambda i: i, lambda j: j, wx_h, wx_l)

    most = wo_h.shape[0]

    def placed(i, height, place_within):
        plane = sum((i >= n * height).astype(jnp.int32) for n in range(1, most // height))
        return plane * 4096 + place_within(i - height * plane)

    def halo_place(i, strip):
        return jnp.where((i >= rows) & (row == 1), i - rows - strip, i)

    def reached(i):
        return jnp.where(i < 8, i + (rows - 8) * (1 - row), halo_place(i - 8 + rows, DATA_STRIP))

    banded(
        1,
        wo_h.shape,
        lambda i: placed(i, used, lambda k: halo_place(k, DATA_STRIP)),
        lambda j: placed(j, rows, lambda k: k),
        wo_h,
        wo_l,
    )
    banded(
        1,
        wr_h.shape,
        lambda i: placed(i, EST_STRIP, reached),
        lambda j: placed(j, EST_STRIP, lambda k: halo_place(k + rows, EST_STRIP)),
        wr_h,
        wr_l,
    )
    banded(
        1,
        wy2_h.shape,
        lambda i: placed(i, pitch, lambda k: jnp.where(k < used, k - DATA_STRIP * row, 1024)),
        lambda j: placed(
            j, pitch, lambda k: jnp.where(k < used, halo_place(k, DATA_STRIP), 2048)
        ),
        wy2_h,
        wy2_l,
    )


def blur_z(read, taps_z):
    taps = [taps_z[t, 0:1, :] for t in range(WIDTH + 1)]
    total = taps[0] * read(WIDTH)
    for t in range(1, WIDTH + 1):
        total = total + taps[t] * (read(WIDTH - t) + read(WIDTH + t))
    return total


def blur_yx(x, w_h, w_l, wx_h, wx_l):
    x_h, x_l = split(x)
    m_h, m_l = split(dot3(w_h, w_l, x_h, x_l))
    return dot3(m_h, m_l, wx_h[...], wx_l[...])


def own_kernel(est, data, est_off, est_on, taps_z, wx_h, wx_l, wo_h, wo_l, out, ratio):
    planes, rows, lanes = est.shape
    wide, used, _ = out.shape
    odd = lax.rem(lax.axis_index("slab"), 2) == 1
    group = 256 // rows

    def work(below, above):
        mids = []
        for start in range(0, wide, group):
            part = [
                blur_z(lambda t: (below, est, above)[(p + t) // planes][(p + t) % planes], taps_z)
                for p in range(start, start + group)
            ]
            x_h, x_l = split(jnp.concatenate(part, axis=0))
            mids.append(split(dot3(wo_h[...], wo_l[...], x_h, x_l)))
        m_h = jnp.concatenate([m[0] for m in mids], axis=0)
        m_l = jnp.concatenate([m[1] for m in mids], axis=0)
        blurred = dot3(m_h, m_l, wx_h[...], wx_l[...]).reshape(wide, used, lanes)
        out[...] = blurred
        ratio[...] = data[:, 8 : rows - 8, :] / blurred[WIDTH : WIDTH + planes, 8 : rows - 8]

    @pl.when(odd)
    def _():
        work(est_on, est_off)

    @pl.when(jnp.logical_not(odd))
    def _():
        work(est_off, est_on)


def views_kernel(
    slabs, partial, inner, data, strip, est_off, off, on,
    taps_z, wx_h, wx_l, wr_h, wr_l, wy2_h, wy2_l, out, rims, ratio, flat,
):
    planes, rows, lanes = data.shape
    slab, row = lax.axis_index("slab"), lax.axis_index("row")
    pitch = rows + EST_STRIP
    used = rows + DATA_STRIP
    wide = planes + 2 * WIDTH
    thick = EST_STRIP + DATA_STRIP
    base = planes * EST_STRIP + WIDTH * DATA_STRIP
    odd = lax.rem(slab, 2) == 1

    def blur_first(below, above):
        def read(q):
            if q // planes == 1:
                return strip[q - planes, 0:EST_STRIP, :]
            at = q % planes * EST_STRIP
            return (below, above)[q // planes // 2][at : at + EST_STRIP, :]

        for p in range(wide):
            rims[p * EST_STRIP : (p + 1) * EST_STRIP, :] = blur_z(lambda t: read(p + t), taps_z)

    @pl.when(odd)
    def _():
        blur_first(on, off)

    @pl.when(jnp.logical_not(odd))
    def _():
        blur_first(off, on)

    mids = []
    reached = blur_yx(rims[...], wr_h[...], wr_l[...], wx_h, wx_l).reshape(wide, 16, lanes)

    def touched(low, high):
        near = reached[low:high, 0:8]
        return (
            partial[low:high, 0:8, :] + jnp.where(row == 1, near, 0.0),
            partial[low:high, rows - 8 : rows, :] + jnp.where(row == 0, near, 0.0),
            partial[low:high, rows:used, :] + reached[low:high, 8:16],
        )

    def beyond(lower):
        next_chip = jnp.logical_not(odd) if lower else odd
        low = 0 if lower else WIDTH + planes
        start, end, last = touched(low, low + WIDTH)
        blurred = jnp.concatenate([start, partial[low : low + WIDTH, 8 : rows - 8, :], end, last], axis=1)
        tops, lows = [], []
        for q in range(WIDTH):
            top = on[base + q * rows : base + (q + 1) * rows, :]
            at = planes * EST_STRIP + q * DATA_STRIP
            at = slice(at, at + DATA_STRIP)
            tops.append(jnp.where(next_chip, est_off[planes + q], top)[None])
            lows.append(jnp.where(next_chip, off[at, :], on[at, :])[None])
        value = [jnp.concatenate(tops, axis=0), jnp.concatenate(lows, axis=0)]
        value = jnp.concatenate(value, axis=1) / blurred
        inside = slab > 0 if lower else slab < slabs - 1
        ratio[low : low + WIDTH] = jnp.where(inside, value, 0.0)

    def second_blur(low, high):
        for p in range(low, high):
            flat[p * pitch : p * pitch + used, :] = blur_z(lambda t: ratio[p + t], taps_z)
            flat[p * pitch + used : (p + 1) * pitch, :] = jnp.zeros((pitch - used, lanes), F32)
        n = (high - low) * pitch
        x_h, x_l = split(flat[low * pitch : low * pitch + n, :])
        return split(dot3(wy2_h[0:n, 0:n], wy2_l[0:n, 0:n], x_h, x_l))

    beyond(True)
    ends = [data[:, 0:8, :], data[:, rows - 8 : rows, :], strip[:, EST_STRIP:thick, :]]
    ends = jnp.concatenate(ends, axis=1) / jnp.concatenate(touched(WIDTH, WIDTH + planes), axis=1)
    own = slice(WIDTH, WIDTH + planes)
    ratio[own, 0:8, :] = ends[:, 0:8]
    ratio[own, 8 : rows - 8, :] = inner[...]
    ratio[own, rows - 8 : used, :] = ends[:, 8:24]
    mids = [second_blur(0, 2), second_blur(2, 4)]
    beyond(False)
    mids += [second_blur(4, 6), second_blur(6, 8)]
    m_h = jnp.concatenate([m[0] for m in mids], axis=0)
    m_l = jnp.concatenate([m[1] for m in mids], axis=0)
    out[...] = dot3(m_h, m_l, wx_h[...], wx_l[...]).reshape(planes, pitch, lanes)[:, :used]


def field_kernel(views, rows, parts, est, strip, out):
    view, row = lax.axis_index("view"), lax.axis_index("row")
    total = parts[0]
    for v in range(1, views):
        total = total + parts[v]
    total = total * (1.0 / views)
    own, rim = est[view], strip[view, 0:EST_STRIP, :]

    @pl.when(row == 0)
    def _():
        value = jnp.concatenate([own * total[0:rows], rim[0:DATA_STRIP] * total[rows:]], axis=0)
        for v in range(views):
            out[v] = value

    @pl.when(row == 1)
    def _():
        value = jnp.concatenate(
            [rim[DATA_STRIP:] * total[0:DATA_STRIP], own * total[DATA_STRIP:]], axis=0
        )
        for v in range(views):
            out[v] = value


def variation_kernel(slabs, rows, field, off, on, out, start, first, second, sems):
    planes, used, lanes = field.shape
    slab, row = lax.axis_index("slab"), lax.axis_index("row")
    half = lanes // 2
    odd = lax.rem(slab, 2)
    start[pl.ds(odd * (planes + TV_HALO), TV_HALO)] = off[...]
    start[pl.ds((1 - odd) * (planes + TV_HALO), TV_HALO)] = on[...]
    start[TV_HALO : TV_HALO + planes] = field[...]
    lane = lax.broadcasted_iota(jnp.int32, (1, 1, half), 2)
    line = lax.broadcasted_iota(jnp.int32, (1, 8, half), 1)

    def next_x(x):
        turned = [pltpu.roll(h, half - 1, 2) for h in x]
        return [
            jnp.where(lane == half - 1, turned[1], turned[0]),
            jnp.where(lane == half - 1, 0.0, turned[1]),
        ]

    def last_x(x):
        turned = [pltpu.roll(h, 1, 2) for h in x]
        return [jnp.where(lane == 0, 0.0, turned[0]), jnp.where(lane == 0, turned[0], turned[1])]

    def next_y(x):
        turned = pltpu.roll(x, used - 1, 1)
        last = jnp.where(line == 7, 0.0, turned[:, used - 8 :])
        return jnp.concatenate([turned[:, : used - 8], last], axis=1)

    def last_y(x):
        turned = pltpu.roll(x, 1, 1)
        return jnp.concatenate([jnp.where(line == 0, 0.0, turned[:, :8]), turned[:, 8:]], axis=1)

    def masked(x, z):
        if z >= TV_HALO and z + x.shape[0] <= TV_HALO + planes:
            return x
        parts = []
        for i in range(x.shape[0]):
            part = x[i : i + 1]
            if z + i < TV_HALO:
                part = jnp.where(slab > 0, part, 0.0)
            elif z + i >= TV_HALO + planes:
                part = jnp.where(slab < slabs - 1, part, 0.0)
            parts.append(part)
        return jnp.concatenate(parts, axis=0) if len(parts) > 1 else parts[0]

    def flux(source, z, count, only_z):
        box = [slice(h * half, (h + 1) * half) for h in range(2)]
        now = [source[z : z + count, :, b] for b in box]
        after = [source[z + 1 : z + count + 1, :, b] for b in box]
        side = next_x(now)
        f_x, f_y, f_z = [], [], []
        for h in range(2):
            g_z, g_y, g_x = after[h] - now[h], next_y(now[h]) - now[h], side[h] - now[h]
            scale = masked(lax.rsqrt(g_z * g_z + g_y * g_y + g_x * g_x + EPS2), z)
            f_z.append(g_z * scale)
            if not only_z:
                f_y.append(g_y * scale)
                f_x.append(g_x * scale)
        return now, f_x, f_y, f_z

    def one_pass(source, low, high, group, target, then=None):
        before = flux(source, low - 1, 1, True)[3]
        for z in range(low, high, group):
            count = min(group, high - z)
            now, f_x, f_y, f_z = flux(source, z, count, False)
            side = last_x(f_x)
            for h in range(2):
                below = before[h]
                if count > 1:
                    below = jnp.concatenate([below, f_z[h][: count - 1]], axis=0)
                spread = (f_z[h] - below) + (f_y[h] - last_y(f_y[h])) + (f_x[h] - side[h])
                target[z : z + count, :, h * half : (h + 1) * half] = masked(now[h] + TAU * spread, z)
            before = [f[count - 1 : count] for f in f_z]
            if then is not None:
                then(z, count)

    deep = planes + 2 * TV_HALO
    groups = (6, 5, 3)
    one_pass(start, 1, deep - 1, groups[0], first)
    one_pass(first, 2, deep - 2, groups[1], second)
    skip = pl.multiple_of(row * (used - rows), 8)
    copies = []

    def leave(z, count):
        copy = pltpu.make_async_copy(
            first.at[z : z + count, pl.ds(skip, rows), :],
            out.at[z - TV_HALO : z - TV_HALO + count],
            sems.at[len(copies)],
        )
        copy.start()
        copies.append(copy)

    one_pass(second, TV_HALO, deep - TV_HALO, groups[2], first, leave)
    for copy in copies:
        copy.wait()


def call(kernel, shapes, scratch, *args, cost=None, scalars=0, target=VMEM):
    specs = [SMEM if i < scalars else VMEM for i in range(len(args))]
    return pl.pallas_call(
        kernel,
        out_shape=shapes,
        in_specs=specs,
        out_specs=jax.tree.map(lambda _: target, shapes),
        scratch_shapes=scratch,
        cost_estimate=cost,
        compiler_params=pltpu.CompilerParams(vmem_limit_bytes=16 * 2**20),
    )(*args)


def body(data, estimate, profile, band, axes_perm):
    data = data[0]
    planes, rows, lanes = estimate.shape
    views, slabs = lax.axis_size("view"), lax.axis_size("slab")
    slab, row = lax.axis_index("slab"), lax.axis_index("row")
    shape = functools.partial(jax.ShapeDtypeStruct, dtype=F32)
    half = functools.partial(jax.ShapeDtypeStruct, dtype=BF16)
    off_pairs = [(i, i + 1) for i in range(1, slabs - 1, 2)]
    off_pairs += [(target, source) for source, target in off_pairs]
    on_pairs = [(i, i ^ 1) for i in range(slabs)]
    odd = lax.rem(slab, 2)

    first_row, is_odd = row == 0, odd == 1
    low = data[:WIDTH].reshape(-1, lanes)
    high = data[planes - WIDTH :].reshape(-1, lanes)
    rim_off, rim_on = jnp.where(is_odd, high, low), jnp.where(is_odd, low, high)
    estimate, data, rim_off, rim_on = lax.optimization_barrier(
        (estimate, data, rim_off, rim_on)
    )
    edge = jnp.concatenate(
        [
            jnp.where(first_row, estimate[:, rows - EST_STRIP :], estimate[:, :EST_STRIP]),
            jnp.where(first_row, data[:, rows - DATA_STRIP :], data[:, :DATA_STRIP]),
        ],
        axis=1,
    )
    strip = lax.ppermute(edge, "row", [(0, 1), (1, 0)])
    held = lax.optimization_barrier((estimate, edge))[0]
    far = jnp.concatenate([held, rim_off.reshape(WIDTH, rows, lanes)], axis=0)
    held, far = lax.optimization_barrier((held, far))
    est_off = lax.ppermute(far, "slab", off_pairs)
    est_on = lax.ppermute(held, "slab", on_pairs)
    parts = [strip[:, :EST_STRIP].reshape(-1, lanes)]
    first = strip[:WIDTH, EST_STRIP:].reshape(-1, lanes)
    last = strip[planes - WIDTH :, EST_STRIP:].reshape(-1, lanes)
    off = jnp.concatenate(parts + [jnp.where(is_odd, last, first)], axis=0)
    on = jnp.concatenate(parts + [jnp.where(is_odd, first, last), rim_on], axis=0)
    off = lax.ppermute(off, "slab", off_pairs)
    on = lax.ppermute(on, "slab", on_pairs)

    pitch, used = rows + EST_STRIP, rows + DATA_STRIP
    wide, group = planes + 2 * WIDTH, 256 // rows
    taps_z, wx_h, wx_l, wo_h, wo_l, wr_h, wr_l, wy2_h, wy2_l = call(
        functools.partial(weights_kernel, rows),
        [shape((WIDTH + 1, 16, lanes))]
        + [half((lanes, lanes))] * 2
        + [half((group * used, group * rows))] * 2
        + [half((wide * EST_STRIP, wide * EST_STRIP))] * 2
        + [half((3 * pitch, 3 * pitch))] * 2,
        [],
        band, axes_perm, profile,
        scalars=3,
        cost=pl.CostEstimate(flops=COST, bytes_accessed=0, transcendentals=0),
    )
    partial, inner = call(
        own_kernel,
        [shape((wide, used, lanes)), shape((planes, rows - 16, lanes))],
        [],
        estimate, data, est_off, est_on, taps_z, wx_h, wx_l, wo_h, wo_l,
    )
    back = call(
        functools.partial(views_kernel, slabs),
        shape((planes, used, lanes)),
        [
            pltpu.VMEM((wide * EST_STRIP, lanes), F32),
            pltpu.VMEM((wide, used, lanes), F32),
            pltpu.VMEM((planes * pitch, lanes), F32),
        ],
        partial, inner, data, strip, est_off, off, on, taps_z, wx_h, wx_l, wr_h, wr_l, wy2_h, wy2_l,
    )
    parts = lax.all_to_all(back, "view", 0, 0, tiled=True)
    copies = call(
        functools.partial(field_kernel, views, rows),
        shape((views, used, lanes)),
        [],
        parts, estimate, strip,
    )
    field = lax.all_to_all(copies, "view", 0, 0, tiled=True)
    reach = planes - TV_HALO
    low, high = field[:TV_HALO], field[reach:]
    off = lax.ppermute(jnp.where(is_odd, high, low), "slab", off_pairs)
    on = lax.ppermute(jnp.where(is_odd, low, high), "slab", on_pairs)
    deep = pltpu.VMEM((planes + 2 * TV_HALO, used, lanes), F32)
    return call(
        functools.partial(variation_kernel, slabs, rows),
        shape((planes, rows, lanes)),
        [deep, deep, deep, pltpu.SemaphoreType.DMA((4,))],
        field, off, on,
        target=pl.BlockSpec(memory_space=pl.ANY),
    )


def solution(mesh):
    placed = (
        P("view", "slab", "row", None),
        P("slab", "row", None),
        P("view", None, None),
        P("view", None),
        P("view", None),
    )
    return jax.shard_map(
        body, mesh=mesh, in_specs=placed, out_specs=P("slab", "row", None), check_vma=False
    )
```
